32 devices in a mesh: dp: 8 (over z, x), tp: 4 (over y, core).
Axes of the slice: x: 2, y: 2, z: 4, core: 2. Of those that a mesh axis runs over, the one named last changes fastest.
Arguments:
- block_input: bfloat16 [32768, 320], P(('dp', 'tp')), may hold values from -6 to 6
- cotangent: bfloat16 [32768, 320], P(('dp', 'tp')), may hold values from -6 to 6
- clip_starts: int32 [16, 4], P('dp'), may hold values from 0 to 1792, as said below
- clip_shapes: int32 [16, 4, 3], P('dp'), may hold values from 1 to 16, as said below
- tile_slot: int32 [60], replicated, may hold values from 0 to 63, as said below
- masters: float32 [4, 64, 16, 320], P('tp', 'dp')
- left_bases: float32 [4, 64, 16, 16], P('tp', 'dp'), as said below
- right_bases: float32 [4, 64, 320, 320], P('tp', 'dp'), as said below
- first_moment: float32 [4, 64, 16, 320], P('tp', 'dp')
- second_moment: float32 [4, 64, 16, 320], P('tp', 'dp'), as said below
- vectors: float32 [40, 320], replicated
- vector_first: float32 [40, 320], replicated
- vector_second: float32 [40, 320], replicated, as said below
- step_count: int32 [1], replicated, may hold values from 2 to 5
Outputs:
- block_output: bfloat16 [32768, 320], P(('dp', 'tp'))
- input_grad: bfloat16 [32768, 320], P(('dp', 'tp'))
- new_masters: float32 [4, 64, 16, 320], P('tp', 'dp')
- new_first: float32 [4, 64, 16, 320], P('tp', 'dp')
- new_second: float32 [4, 64, 16, 320], P('tp', 'dp')
- new_vectors: float32 [40, 320], replicated
- new_vector_first: float32 [40, 320], replicated
- new_vector_second: float32 [40, 320], replicated
The draws below stay inside these ranges and needn't reach their ends.
Inputs may be any that keep to these rules, and one draw needn't show every extreme that they name: `clip_starts`: starts of each packed sequence's clips in increasing order: the first is 0, each clip ends where the next begins and the last at 2048; the clips hold 1024, 512, 256 and 256 tokens in some order. `clip_shapes`: height and width are each 16 or 8; frames times height times width is the clip's token count; tokens run frame by frame, row by row. `tile_slot`: all different; slots 0 and 63 are always named. `left_bases`: each slot's basis is orthogonal. `right_bases`: each slot's basis is orthogonal. `second_moment`: Positive. `vector_second`: Positive.
All inputs are finite; a program needn't handle non-finite values.
Results may differ from the reference program's by a relative error of at most 0.014.
Values may be sent and summed in bfloat16 or wider, within the bound.
No kernel may reach another device: no remote copies, remote signals or barrier semaphores. Data moves between devices by JAX's collectives and lax.ppermute only.
A program may use at most 192 MiB of HBM per device.

```python
import math
import jax
import jax.numpy as jnp
from jax import lax

D = 320
HEADS = 5
HD = 64
FF = 1280
SEQ = 2048
SIDE = 16
CLIPS = 4
TR = 16
SLOTS = 64
TILES = 60
NVEC = 40
NSEQ = 16
TOKENS = 32768


def slot_list(key):
    inner = jax.random.fold_in(key, 7)
    first_key, second_key = jax.random.split(inner)
    empty = 1 + jax.random.permutation(first_key, SLOTS - 2)[:SLOTS - TILES]
    marks = jnp.zeros((SLOTS,), jnp.int32).at[empty].set(1)
    score = jax.random.permutation(second_key, SLOTS).astype(jnp.int32) + SLOTS * marks
    return jnp.argsort(score, stable=True)[:TILES].astype(jnp.int32)


def slot_kinds(key):
    order = slot_list(key)
    owner = jnp.full((SLOTS,), -1, jnp.int32).at[order].set(jnp.arange(TILES, dtype=jnp.int32))
    groups = FF // D
    hidden_part = FF // groups
    first_row = owner[None, :] * TR
    group_ids = jnp.arange(groups, dtype=jnp.int32)[:, None]
    attention_row = group_ids * D + first_row
    attention_kind = attention_row % (4 * HD) // HD
    kind = jnp.where(first_row < D, attention_kind, jnp.where(first_row < D + hidden_part, 4, 5))
    kind = jnp.where(owner[None, :] < 0, 6, kind)
    return kind


def noise_of(key, shape):
    return jnp.clip(jax.random.normal(key, shape, jnp.float32), -5.0, 5.0)


def clip_layout(key):
    inner = jax.random.fold_in(key, 3)
    order_key, height_key, width_key = jax.random.split(inner, 3)
    count = NSEQ
    base_sizes = jnp.array([SEQ // 2, SEQ // 4, SEQ // 8, SEQ // 8], jnp.int32)
    ranks = jax.vmap(lambda item: jax.random.permutation(item, CLIPS))(jax.random.split(order_key, count)).astype(jnp.int32)
    lead_row = jnp.concatenate([jax.random.permutation(jax.random.fold_in(order_key, 5), 3).astype(jnp.int32), jnp.array([3], jnp.int32)])
    ranks = ranks.at[0].set(lead_row)
    sizes = base_sizes[ranks]
    starts = (jnp.cumsum(sizes, axis=1) - sizes).astype(jnp.int32)
    height = jnp.where(jax.random.randint(height_key, (count, CLIPS), 0, 2) == 1, SIDE, SIDE // 2).astype(jnp.int32)
    width = jnp.where(jax.random.randint(width_key, (count, CLIPS), 0, 2) == 1, SIDE, SIDE // 2).astype(jnp.int32)
    height = height.at[0].set(jnp.where(ranks[0] == 0, SIDE // 2, jnp.where(ranks[0] == 3, SIDE, height[0])).astype(jnp.int32))
    width = width.at[0].set(jnp.where(ranks[0] == 0, SIDE // 2, jnp.where(ranks[0] == 3, SIDE, width[0])).astype(jnp.int32))
    frames = (sizes // (height * width)).astype(jnp.int32)
    return (starts, jnp.stack([frames, height, width], axis=-1))


def draw_clip_starts(key, part):
    return clip_layout(key)[0]


def draw_clip_shapes(key, part):
    return clip_layout(key)[1]


def draw_tile_slot(key, part):
    return slot_list(key)


def draw_masters(key, part):
    kind = slot_kinds(key)
    table = jnp.array([2.5 * (4.0 * D) ** (-0.5), 2.5 * (4.0 * D) ** (-0.5), D ** (-0.5), (D / 8.0) ** (-0.5), D ** (-0.5), FF ** (-0.5), D ** (-0.5)], jnp.float32)
    scale = jnp.take(table, kind)
    noise = noise_of(jax.random.fold_in(key, 21), (FF // D, SLOTS, TR, D))
    return noise * scale[:, :, None, None]


def orthogonal(key, shape):
    matrix = jax.random.normal(key, shape, jnp.float32)
    factor_q, factor_r = jnp.linalg.qr(matrix)
    signs = jnp.where(jnp.diagonal(factor_r, axis1=-2, axis2=-1) < 0, -1.0, 1.0)
    return factor_q * signs[..., None, :]


def draw_left_bases(key, part):
    return orthogonal(jax.random.fold_in(key, 31), (FF // D, SLOTS, TR, TR))


def draw_right_bases(key, part):
    return orthogonal(jax.random.fold_in(key, 41), (FF // D, SLOTS, D, D))


def grad_sizes(key):
    kind = slot_kinds(key)
    table = jnp.array([1.125, 1.125, 0.9, 0.3, 0.3, 0.6, 0.5], jnp.float32) * math.sqrt(TOKENS)
    return jnp.take(table, kind)[:, :, None, None]


def draw_first_moment(key, part):
    first_key, second_key = jax.random.split(jax.random.fold_in(key, 51))
    shape = (FF // D, SLOTS, TR, D)
    signs = jnp.where(jax.random.uniform(first_key, shape) < 0.5, -1.0, 1.0)
    size = jnp.exp(jax.random.uniform(second_key, shape, jnp.float32, math.log(0.5), math.log(2.0)))
    return signs * size * ((1.0 - 0.9) / 0.9) * grad_sizes(key)


def draw_second_moment(key, part):
    shape = (FF // D, SLOTS, TR, D)
    inner = jax.random.fold_in(key, 61)
    size = jnp.exp(jax.random.uniform(inner, shape, jnp.float32, 0.0, math.log(4.0)))
    scale = grad_sizes(key)
    return size * ((1.0 - 0.99) / 0.99) * scale * scale


def draw_vectors(key, part):
    rows = jnp.arange(NVEC, dtype=jnp.int32)[:, None]
    noise = noise_of(jax.random.fold_in(key, 71), (NVEC, D))
    gains = (rows == 28) | (rows == 33)
    return jnp.where(rows < 27, noise / math.sqrt(27.0), jnp.where(gains, 1.0 + 0.08 * noise, 0.3 * noise))


def draw_vector_first(key, part):
    first_key, second_key = jax.random.split(jax.random.fold_in(key, 81))
    shape = (NVEC, D)
    signs = jnp.where(jax.random.uniform(first_key, shape) < 0.5, -1.0, 1.0)
    size = jnp.exp(jax.random.uniform(second_key, shape, jnp.float32, math.log(0.5), math.log(2.0)))
    return signs * size * ((1.0 - 0.9) / 0.9) * math.sqrt(TOKENS)


def draw_vector_second(key, part):
    inner = jax.random.fold_in(key, 91)
    size = jnp.exp(jax.random.uniform(inner, (NVEC, D), jnp.float32, 0.0, math.log(4.0)))
    return size * ((1.0 - 0.99) / 0.99) * TOKENS


def shard_levels(rng, dims, shards, smallest, largest):
    level, own = 1.0, jax.random.fold_in(rng, 6)
    for axis_at, parts in shards:
        steps = jnp.exp(jax.random.uniform(jax.random.fold_in(own, axis_at), (parts,), jnp.float32, smallest / len(shards), largest / len(shards)))
        level = level * jnp.repeat(steps, dims[axis_at] // parts).reshape([-1 if axis == axis_at else 1 for axis in range(len(dims))])
    return level


def gaussian(own_key, dims, spread, bound, cuts=(), kind=jnp.bfloat16):
    values = spread * jax.random.normal(own_key, dims, jnp.float32)
    if cuts:
        values = values * shard_levels(own_key, dims, cuts, -0.22, 0.18)
    return jnp.clip(values, -bound, bound).astype(kind)


def setup_inputs(seed: int = 0) -> dict:
    keys = jax.random.split(jax.random.key(seed), 15)
    block_input = gaussian(keys[0], (TOKENS, D), 1.0, 6.0, ((0, 32),))
    cotangent = gaussian(keys[1], (TOKENS, D), 1.0, 6.0, ((0, 32),))
    clip_starts = draw_clip_starts(jax.random.fold_in(keys[14], 71), 0)
    clip_shapes = draw_clip_shapes(jax.random.fold_in(keys[14], 71), 0)
    tile_slot = draw_tile_slot(jax.random.fold_in(keys[14], 71), 0)
    masters = draw_masters(jax.random.fold_in(keys[14], 71), 0)
    left_bases = draw_left_bases(jax.random.fold_in(keys[14], 71), 0)
    right_bases = draw_right_bases(jax.random.fold_in(keys[14], 71), 0)
    first_moment = draw_first_moment(jax.random.fold_in(keys[14], 71), 0)
    second_moment = draw_second_moment(jax.random.fold_in(keys[14], 71), 0)
    vectors = draw_vectors(jax.random.fold_in(keys[14], 71), 0)
    vector_first = draw_vector_first(jax.random.fold_in(keys[14], 71), 0)
    vector_second = draw_vector_second(jax.random.fold_in(keys[14], 71), 0)
    step_count = jax.random.randint(keys[13], (1,), 2, 6).astype(jnp.int32)
    return {"block_input": block_input, "cotangent": cotangent, "clip_starts": clip_starts, "clip_shapes": clip_shapes, "tile_slot": tile_slot, "masters": masters, "left_bases": left_bases, "right_bases": right_bases, "first_moment": first_moment, "second_moment": second_moment, "vectors": vectors, "vector_first": vector_first, "vector_second": vector_second, "step_count": step_count}


highest = lax.Precision.HIGHEST
norm_eps = 1e-06
beta_one = 0.9
beta_two = 0.99
adam_eps = 1e-08
matrix_rate = 0.1
matrix_decay = 0.05
vector_rate = 0.5
masked_score = -1e+30

@jax.custom_vjp
def low(v):
    return lax.optimization_barrier(v.astype(jnp.bfloat16)).astype(jnp.float32)

@jax.custom_vjp
def low_back(v):
    return v

def low_keep(v):
    return (low(v), None)

def low_pass(kept, grad):
    return (grad,)

def back_keep(v):
    return (v, None)

def back_low(kept, grad):
    return (low(grad),)
low.defvjp(low_keep, low_pass)
low_back.defvjp(back_keep, back_low)

def geometry(starts, shapes, seq_len):
    count = starts.shape[0]
    clips = starts.shape[1]
    place = jnp.arange(seq_len, dtype=jnp.int32)
    member = (place[None, :, None] >= starts[:, None, :]).astype(jnp.int32)
    which = lax.optimization_barrier(jnp.sum(member, axis=-1)).astype(jnp.int32) - 1
    onehot = (which[:, :, None] == jnp.arange(clips, dtype=jnp.int32)[None, None, :]).astype(jnp.int32)
    begin = lax.optimization_barrier(jnp.sum(onehot * starts[:, None, :], axis=-1)).astype(jnp.int32)
    frames = lax.optimization_barrier(jnp.sum(onehot * shapes[:, None, :, 0], axis=-1)).astype(jnp.int32)
    height = lax.optimization_barrier(jnp.sum(onehot * shapes[:, None, :, 1], axis=-1)).astype(jnp.int32)
    width = lax.optimization_barrier(jnp.sum(onehot * shapes[:, None, :, 2], axis=-1)).astype(jnp.int32)
    local = place[None, :] - begin
    plane = height * width
    frame_at = local // plane
    row_at = local // width % height
    column_at = local % width
    base = jnp.arange(count, dtype=jnp.int32)[:, None] * seq_len + place[None, :]
    label = jnp.arange(count, dtype=jnp.int32)[:, None] * clips + which
    targets = []
    valids = []
    for frame_step in (-1, 0, 1):
        for row_step in (-1, 0, 1):
            for column_step in (-1, 0, 1):
                inside = (frame_at + frame_step >= 0) & (frame_at + frame_step < frames)
                inside = inside & (row_at + row_step >= 0) & (row_at + row_step < height)
                inside = inside & (column_at + column_step >= 0) & (column_at + column_step < width)
                target = base + frame_step * plane + row_step * width + column_step
                targets.append(jnp.where(inside, target, base).reshape(-1).astype(jnp.int32))
                valids.append(inside.reshape(-1))
    return (jnp.stack(targets), jnp.stack(valids), label.reshape(-1).astype(jnp.int32))

def layer_norm(values, gain, shift):
    center = values - lax.optimization_barrier(jnp.mean(values, axis=-1, keepdims=True))
    return center * lax.rsqrt(lax.optimization_barrier(jnp.mean(center * center, axis=-1, keepdims=True)) + norm_eps) * gain + shift

def forward(attention_table, fc_one, fc_two, vectors, inputs, taps, valid, label):
    first = inputs + vectors[27]
    for tap in range(27):
        first = first + jnp.where(valid[tap][:, None], jnp.take(inputs, taps[tap], axis=0) * vectors[tap], 0.0)
    attend_in = low(layer_norm(first, vectors[28], vectors[29]))
    table = attention_table.reshape(HEADS, 4, HD, D)
    query = jnp.einsum('td,hjd->htj', attend_in, table[:, 0], precision=highest) + vectors[30].reshape(HEADS, 1, HD)
    key = jnp.einsum('td,hjd->htj', attend_in, table[:, 1], precision=highest)
    value = jnp.einsum('td,hjd->htj', attend_in, table[:, 2], precision=highest) + vectors[31].reshape(HEADS, 1, HD)
    query = low(low_back(query))
    key = low(low_back(key))
    value = low(low_back(value))
    scores = low_back(jnp.einsum('hqj,hkj->hqk', query, key, precision=highest) * (1.0 / math.sqrt(HD)))
    same = label[:, None] == label[None, :]
    scores = jnp.where(same[None], scores, masked_score)
    peak = lax.optimization_barrier(jnp.max(scores, axis=-1, keepdims=True))
    weights = jnp.exp(scores - peak)
    probs = weights / lax.optimization_barrier(jnp.sum(weights, axis=-1, keepdims=True))
    heads_out = low(low_back(jnp.einsum('hqk,hkj->hqj', low(probs), value, precision=highest)))
    projected = jnp.einsum('hqj,hjd->qd', heads_out, table[:, 3], precision=highest)
    second = first + low_back(projected + vectors[32])
    mlp_in = low(layer_norm(second, vectors[33], vectors[34]))
    fc_one_bias = vectors[35:35 + FF // D].reshape(FF)
    pre = low_back(jnp.dot(mlp_in.astype(jnp.float32), fc_one.T.astype(jnp.float32), precision=highest, preferred_element_type=jnp.float32) + fc_one_bias)
    hidden = low(jax.nn.gelu(pre, approximate=False))
    return second + jnp.dot(hidden.astype(jnp.float32), fc_two.astype(jnp.float32), precision=highest, preferred_element_type=jnp.float32) + vectors[35 + FF // D]

def soap_update(masters, left, right, first, second, grad, steps):
    rotated = jnp.einsum('gsia,gsib->gsab', left, grad, precision=highest)
    rotated = jnp.einsum('gsab,gsbc->gsac', rotated, right, precision=highest)
    new_first = beta_one * first + (1.0 - beta_one) * rotated
    new_second = beta_two * second + (1.0 - beta_two) * rotated * rotated
    corr_one = 1.0 - jnp.power(beta_one, steps)
    corr_two = 1.0 - jnp.power(beta_two, steps)
    direction = new_first / corr_one / (jnp.sqrt(new_second / corr_two) + adam_eps)
    back = jnp.einsum('gsia,gsab->gsib', left, direction, precision=highest)
    back = jnp.einsum('gsib,gscb->gsic', back, right, precision=highest)
    return (masters - matrix_rate * (back + matrix_decay * masters), new_first, new_second)

def vector_update(values, first, second, grad, steps):
    new_first = beta_one * first + (1.0 - beta_one) * grad
    new_second = beta_two * second + (1.0 - beta_two) * grad * grad
    corr_one = 1.0 - jnp.power(beta_one, steps)
    corr_two = 1.0 - jnp.power(beta_two, steps)
    direction = new_first / corr_one / (jnp.sqrt(new_second / corr_two) + adam_eps)
    return (values - vector_rate * direction, new_first, new_second)

def reference(block_input, cotangent, clip_starts, clip_shapes, tile_slot, masters, left_bases, right_bases, first_moment, second_moment, vectors, vector_first, vector_second, step_count):
    groups = FF // D
    hidden_part = FF // groups
    weights = low(masters)
    logical = weights[:, tile_slot].reshape(groups, TILES * TR, D)
    attention_table = logical[:, :D].reshape(groups * D, D)
    fc_one = logical[:, D:D + hidden_part].reshape(FF, D)
    fc_two = logical[:, D + hidden_part:].reshape(FF, D)
    sequences = clip_starts.shape[0]
    inputs = block_input.astype(jnp.float32).reshape(sequences, SEQ, D)
    cotan = cotangent.astype(jnp.float32).reshape(sequences, SEQ, D)

    def accumulate(totals, item):
        seq_in, seq_cot, starts, shapes = item
        taps, valid, label = geometry(starts[None], shapes[None], SEQ)

        def run(table, one, two, vec, values):
            return forward(table, one, two, vec, values, taps, valid, label)
        result, pullback = jax.vjp(run, attention_table, fc_one, fc_two, vectors, seq_in)
        grads = pullback(seq_cot)
        totals = (totals[0] + grads[0], totals[1] + grads[1], totals[2] + grads[2], totals[3] + grads[3])
        return (totals, (result.astype(jnp.bfloat16), grads[4].astype(jnp.bfloat16)))
    zeros = (jnp.zeros_like(attention_table), jnp.zeros_like(fc_one), jnp.zeros_like(fc_two), jnp.zeros_like(vectors))
    totals, outs = lax.scan(accumulate, zeros, (inputs, cotan, clip_starts, clip_shapes))
    block_output = outs[0].reshape(sequences * SEQ, D)
    input_grad = outs[1].reshape(sequences * SEQ, D)
    grad_table, grad_one, grad_two, grad_vectors = totals
    per_group = jnp.concatenate([grad_table.reshape(groups, D, D), grad_one.reshape(groups, hidden_part, D), grad_two.reshape(groups, hidden_part, D)], axis=1)
    per_group = per_group.reshape(groups, TILES, TR, D)
    tile_grad = jnp.zeros(masters.shape, jnp.float32).at[:, tile_slot].set(per_group)
    steps = step_count[0].astype(jnp.float32)
    new_masters, new_first, new_second = soap_update(masters, left_bases, right_bases, first_moment, second_moment, tile_grad, steps)
    new_vectors, new_vector_first, new_vector_second = vector_update(vectors, vector_first, vector_second, grad_vectors, steps)
    return (block_output, input_grad, new_masters, new_first, new_second, new_vectors, new_vector_first, new_vector_second)
```

```python
import functools

import jax
import jax.numpy as jnp
from jax import lax
from jax.experimental import pallas as pl
from jax.experimental.pallas import tpu as pltpu
from jax.sharding import PartitionSpec as P

D = 320
DP = 384
HEADS = 5
HD = 64
FF = 1280
SEQ = 2048
HALF = SEQ // 2
TR = 16
SLOTS = 64
TILES = 60
NVEC = 40
GROUPS = FF // D

norm_eps = 1e-06
beta_one = 0.9
beta_two = 0.99
adam_eps = 1e-08
matrix_rate = 0.1
matrix_decay = 0.05
vector_rate = 0.5

SIZES = (1024, 512, 256, 256)
CANON = (0, 1024, 1536, 1792)
GAP = 34
PTILES = (GAP, 2 * GAP + 128, 3 * GAP + 192, 4 * GAP + 224)
ALL_TILES = 5 * GAP + 256
WIDTHS = (128, 128, 64)

f32 = jnp.float32
bf16 = jnp.bfloat16
NN = (((1,), (0,)), ((), ()))
NT = (((1,), (1,)), ((), ()))
TN = (((0,), (0,)), ((), ()))

SMEM = pl.BlockSpec(memory_space=pltpu.SMEM)
VMEM = pl.BlockSpec(memory_space=pltpu.VMEM)
ANY = pl.BlockSpec(memory_space=pl.ANY)


def dot(a, b, dims):
    return lax.dot_general(a, b, dims, preferred_element_type=f32)


def mult(value, step):
    return pl.multiple_of(value, step)


META_STARTS = 1
META_SHAPES = 9
META_TILES = 33


def layout_of(meta):
    part = meta[0]
    core = lax.rem(part, 2)
    row = lax.div(part, 2)
    starts = [meta[META_STARTS + row * 4 + i] for i in range(4)]
    shapes = [[meta[META_SHAPES + row * 12 + 3 * i + k] for k in range(3)] for i in range(4)]
    counts = [s[0] * s[1] * s[2] for s in shapes]
    seen = jnp.int32(0)
    marks = [[], [], [], []]
    for i in range(4):
        small = (counts[i] == 256).astype(jnp.int32)
        marks[0].append((counts[i] == 1024).astype(jnp.int32))
        marks[1].append((counts[i] == 512).astype(jnp.int32))
        marks[2].append(small * (1 - seen))
        marks[3].append(small * seen)
        seen = jnp.maximum(seen, small)
    clips = []
    for mark in marks:
        pick = lambda values: sum(m * v for m, v in zip(mark, values))
        clips.append((pick(starts), pick([s[1] for s in shapes]), pick([s[2] for s in shapes])))
    return core, clips


def own_pieces(core, clips):
    small_start = jnp.where(core == 0, clips[2][0], clips[3][0])
    return (
        (512, 0, core * 512, clips[0][0] + core * 512),
        (256, 512, 1024 + core * 256, clips[1][0] + core * 256),
        (256, 768, 1536 + core * 256, small_start),
    )


def pair_copies(core, own, other, into, sem):
    first = pltpu.make_async_copy(own, into.at[pl.ds(mult(core * HALF, HALF), HALF)], sem.at[0])
    second = pltpu.make_async_copy(
        other, into.at[pl.ds(mult((1 - core) * HALF, HALF), HALF)], sem.at[1]
    )
    return first, second


def clear_gaps(x0, xm, xp):
    for ref in (x0, xm, xp):
        for at in (0,) + tuple(p + s // 8 for p, s in zip(PTILES, SIZES)):
            ref[:, at : at + GAP] = jnp.zeros((3, GAP, 8, 128), f32)
        ref[2, :, :, 64:128] = jnp.zeros((ALL_TILES, 8, 64), f32)


def put_shifted(x0, xm, xp, chunk, tile, value, clip_width):
    rows, width = value.shape
    column = lax.broadcasted_iota(jnp.int32, (rows, width), 0) & (clip_width - 1)
    left = jnp.where(column != 0, pltpu.roll(value, 1, 0), 0.0)
    right = jnp.where(column != clip_width - 1, pltpu.roll(value, rows - 1, 0), 0.0)
    at = pl.ds(tile, rows // 8)
    lanes = slice(0, width)
    x0[chunk, at, :, lanes] = value.reshape(rows // 8, 8, width)
    xm[chunk, at, :, lanes] = left.reshape(rows // 8, 8, width)
    xp[chunk, at, :, lanes] = right.reshape(rows // 8, 8, width)


def tap_rows(vec, vb):
    for k in range(27):
        for c in range(3):
            vb[k, c] = jnp.broadcast_to(vec[k : k + 1, c * 128 : c * 128 + 128], (8, 128))


def conv_kernel(meta, x_own, x_oth, vec, attend, first, xs, x0, xm, xp, vb, sem):
    core, clips = layout_of(meta)
    copies = pair_copies(core, x_own, x_oth, xs, sem)
    for copy in copies:
        copy.start()
    clear_gaps(x0, xm, xp)
    tap_rows(vec, vb)
    for copy in copies:
        copy.wait()
    for i in range(4):
        for b in range(SIZES[i] // 256):
            row = mult(clips[i][0] + b * 256, 256)
            for c in range(3):
                value = xs[pl.ds(row, 256), c * 128 : c * 128 + WIDTHS[c]].astype(f32)
                put_shifted(x0, xm, xp, c, PTILES[i] + b * 32, value, clips[i][2])
    lane = lax.broadcasted_iota(jnp.int32, (8, 8, 128), 2)
    at_tile = lax.broadcasted_iota(jnp.int32, (8, 8, 128), 0)

    def unit(u, carry):
        i = (u >= 16).astype(jnp.int32) + (u >= 24).astype(jnp.int32) + (u >= 28).astype(jnp.int32)
        pick = lambda values: jnp.where(
            i == 0, values[0], jnp.where(i == 1, values[1], jnp.where(i == 2, values[2], values[3]))
        )
        width = lax.div(pick([c[2] for c in clips]), 8)
        plane = pick([c[1] for c in clips]) * width
        tile = u * 8 + GAP * (i + 1)
        place = (at_tile + u * 8) & (plane - 1)
        inside = (place >= width, None, place < plane - width)
        sums = []
        for c in range(3):
            total = x0[c, pl.ds(tile, 8)] + vec[27:28, c * 128 : c * 128 + 128]
            for dr in range(3):
                part = None
                for df in range(3):
                    at = pl.ds(tile + (df - 1) * plane + (dr - 1) * width, 8)
                    for dc, ref in enumerate((xm, x0, xp)):
                        term = ref[c, at] * vb[9 * df + 3 * dr + dc, c]
                        part = term if part is None else part + term
                if dr != 1:
                    part = jnp.where(inside[dr], part, 0.0)
                total = total + part
            sums.append(total)
        rows = pl.ds(mult(u * 64, 64), 64)
        for c in range(3):
            first[rows, c * 128 : c * 128 + 128] = sums[c].reshape(64, 128)
        mean = jnp.sum(sums[0] + sums[1] + sums[2], axis=-1, keepdims=True) * (1.0 / D)
        center = [s - mean for s in sums]
        center[2] = jnp.where(lane < 64, center[2], 0.0)
        square = center[0] * center[0] + center[1] * center[1] + center[2] * center[2]
        scale = lax.rsqrt(jnp.sum(square, axis=-1, keepdims=True) * (1.0 / D) + norm_eps)
        for c in range(3):
            lanes = slice(c * 128, c * 128 + 128)
            out = center[c] * scale * vec[28:29, lanes] + vec[29:30, lanes]
            attend[rows, lanes] = out.reshape(64, 128).astype(bf16)
        return carry

    lax.fori_loop(0, SEQ // 64, unit, 0)


def conv_forward(meta, x_own, x_oth, vec):
    return pl.pallas_call(
        conv_kernel,
        out_shape=(
            jax.ShapeDtypeStruct((SEQ, DP), bf16),
            jax.ShapeDtypeStruct((SEQ, DP), f32),
        ),
        in_specs=[SMEM, ANY, ANY, VMEM],
        out_specs=(VMEM, VMEM),
        scratch_shapes=[
            pltpu.VMEM((SEQ, D), bf16),
            pltpu.VMEM((3, ALL_TILES, 8, 128), f32),
            pltpu.VMEM((3, ALL_TILES, 8, 128), f32),
            pltpu.VMEM((3, ALL_TILES, 8, 128), f32),
            pltpu.VMEM((27, 3, 8, 128), f32),
            pltpu.SemaphoreType.DMA((2,)),
        ],
        compiler_params=pltpu.CompilerParams(vmem_limit_bytes=48 * 2**20),
        cost_estimate=pl.CostEstimate(flops=2 * 10**9, bytes_accessed=8 * 10**6, transcendentals=0),
        name="conv_forward",
    )(meta, x_own, x_oth, vec)


def norm_parts(values, mask):
    mean = jnp.sum(values, axis=-1, keepdims=True) * (1.0 / D)
    center = jnp.where(mask, values - mean, 0.0)
    scale = lax.rsqrt(jnp.sum(center * center, axis=-1, keepdims=True) * (1.0 / D) + norm_eps)
    return center * scale, scale


def norm_back(grad, normed, scale, gain):
    scaled = grad * gain
    mean = jnp.sum(scaled, axis=-1, keepdims=True) * (1.0 / D)
    inner = jnp.sum(scaled * normed, axis=-1, keepdims=True) * (1.0 / D)
    return scale * (scaled - mean - normed * inner)


def phi_parts(v):
    density = jnp.exp(v * v * -0.5) * 0.3989422804014327
    base = 1.0 + 0.2316419 * jnp.abs(v)
    t = pl.reciprocal(base, approx=True)
    t = t * (2.0 - base * t)
    poly = 1.330274429
    for factor in (-1.821255978, 1.781477937, -0.356563782, 0.319381530):
        poly = poly * t + factor
    upper = density * (poly * t)
    return jnp.where(v >= 0.0, 1.0 - upper, upper), density


SEGMENTS = ((0, 512, 0, 1024), (512, 256, 1024, 512), (768, 256, 1536, 256))


def forward_kernel(
    meta,
    attend,
    first,
    vec,
    bias_qv,
    bias_one,
    w0,
    w1,
    w2,
    w3,
    cot_own,
    cot_oth,
    prob_a,
    prob_b,
    prob_c,
    keys_out,
    query_out,
    heads_out,
    table,
    block_out,
    grad_second,
    branch,
    grads_send,
    grads_keep,
    rows_out,
    fc_rows,
    second,
    cots,
    fc_one,
    fc_two,
    hidden,
    grad_pre,
    mlp_in,
    cot_low,
    grads,
    sem,
):
    core, clips = layout_of(meta)
    part = meta[0]
    pieces = own_pieces(core, clips)
    copies = list(pair_copies(core, cot_own, cot_oth, cots, sem))
    for n, (count, at, canon, _) in enumerate(pieces):
        copies.append(
            pltpu.make_async_copy(
                first.at[pl.ds(mult(canon, 256), count)], second.at[pl.ds(at, count)], sem.at[2 + n]
            )
        )
    for copy in copies:
        copy.start()

    for ref in (table, fc_one, fc_two):
        ref[:, 256:DP] = jnp.zeros((FF, 128), bf16)
    for q, source in enumerate((w0, w1, w2, w3)):
        group = jnp.bitwise_xor(part, q)
        for kind, ref in enumerate((table, fc_one, fc_two)):

            def move(j, carry, source=source, group=group, kind=kind, ref=ref):
                slot = meta[META_TILES + kind * 20 + j]
                ref[pl.ds(mult(group * D + j * TR, TR), TR), 0:D] = source[slot]
                return carry

            lax.fori_loop(0, D // TR, move, 0)
    for copy in copies:
        copy.wait()

    second[...] = second[...] + vec[32:33, :]
    low_lane = lax.broadcasted_iota(jnp.int32, (1, 128), 1) < HD

    def head(h, carry):
        base = mult(h * 4 * HD, 4 * HD)
        bias = bias_qv[h]
        w_query = table[pl.ds(base, 128), :]
        w_keys = table[pl.ds(base + HD, 128), :]
        bias_q = jnp.where(low_lane, bias, 0.0)
        bias_v = bias - bias_q
        keys_out[h, 0:1536] = (dot(attend[0:1536, :], w_keys, NT) + bias_v).astype(bf16)
        small = attend[pl.ds(mult(1536 + core * 256, 256), 256), :]
        keys_out[h, 1536:1792] = (dot(small, w_keys, NT) + bias_v).astype(bf16)
        for count, at, canon, _ in pieces:
            value = dot(attend[pl.ds(mult(canon, 256), count), :], w_query, NT) + bias_q
            value = jnp.where(low_lane, value, 0.0).astype(bf16) * bf16(0.125)
            query_out[h, at : at + count] = value
        for (q_at, q_rows, k_at, k_rows), prob in zip(SEGMENTS, (prob_a, prob_b, prob_c)):
            keys = keys_out[h, k_at : k_at + k_rows]
            step = min(q_rows, 256)
            for at in range(0, q_rows, step):
                scores = dot(query_out[h, q_at + at : q_at + at + step], keys, NT)
                weights = jnp.exp(scores - jnp.max(scores, axis=-1, keepdims=True))
                inverse = 1.0 / jnp.sum(weights, axis=-1, keepdims=True)
                probs = (weights * inverse).astype(bf16)
                prob[h, at : at + step] = probs
                out = jnp.where(low_lane, 0.0, dot(probs, keys, NN)).astype(bf16)
                heads_out[h, q_at + at : q_at + at + step] = out
        second[...] += dot(heads_out[h], table[pl.ds(base + 128, 128), :], NN)
        return carry

    lax.fori_loop(0, HEADS, head, 0)

    mask = lax.broadcasted_iota(jnp.int32, (1, DP), 1) < D
    rows_out[...] = jnp.zeros_like(rows_out)
    fc_rows[...] = jnp.zeros_like(fc_rows)
    cot_low[:, 256:DP] = jnp.zeros((HALF, 128), bf16)

    places = [pieces[0][3], pieces[0][3] + 256, pieces[1][3], pieces[2][3]]

    def chunk(n, carry):
        at = mult(n * 256, 256)
        rows = pl.ds(at, 256)
        place = jnp.where(
            n == 0, places[0], jnp.where(n == 1, places[1], jnp.where(n == 2, places[2], places[3]))
        )
        cot_low[rows, 0:D] = cots[pl.ds(mult(place, 256), 256), :]
        cot = cot_low[rows, :]
        cot_wide = cot.astype(f32)
        after = second[rows, :]
        normed, scale = norm_parts(after, mask)
        inner = (normed * vec[33:34, :] + vec[34:35, :]).astype(bf16)
        mlp_in[rows, :] = inner
        for f in range(0, FF, 256):
            lanes = slice(f, f + 256)
            pre = dot(inner, fc_one[lanes, :], NT) + bias_one[:, lanes]
            below, density = phi_parts(pre)
            hidden[rows, lanes] = (pre * below).astype(bf16)
            back = dot(cot, fc_two[lanes, :], NT) * (below + pre * density)
            back_low = back.astype(bf16)
            grad_pre[rows, lanes] = back_low
            fc_rows[0:1, lanes] += jnp.sum(back_low.astype(f32), axis=0, keepdims=True)
        result = after + dot(hidden[rows, :], fc_two[...], NN) + vec[39:40, :]
        block_out[rows, :] = result[:, 0:D].astype(bf16)
        grad_in = dot(grad_pre[rows, :], fc_one[...], NN)
        rows_out[33:34, :] += jnp.sum(grad_in * normed, axis=0, keepdims=True)
        rows_out[34:35, :] += jnp.sum(grad_in, axis=0, keepdims=True)
        rows_out[39:40, :] += jnp.sum(cot_wide, axis=0, keepdims=True)
        whole = cot_wide + norm_back(grad_in, normed, scale, vec[33:34, :])
        whole = jnp.where(mask, whole, 0.0)
        grad_second[rows, :] = whole
        low = whole.astype(bf16)
        branch[rows, :] = low
        rows_out[32:33, :] += jnp.sum(low.astype(f32), axis=0, keepdims=True)
        return carry

    lax.fori_loop(0, 4, chunk, 0)

    for kind, (left, right) in enumerate(((grad_pre, mlp_in), (hidden, cot_low))):
        grads[...] = dot(left[...], right[...], TN)[:, 0:D]
        for q in range(4):
            value = grads[pl.ds(mult(jnp.bitwise_xor(part, q) * D, 64), D), :]
            if q % 2:
                grads_send[q // 2, kind * D : kind * D + D] = value.astype(bf16)
            else:
                grads_keep[q // 2, kind * D : kind * D + D] = value


def forward_block(meta, attend, first, vec, bias_qv, bias_one, weights, cot_own, cot_oth):
    return pl.pallas_call(
        forward_kernel,
        out_shape=(
            jax.ShapeDtypeStruct((HEADS, 512, 1024), bf16),
            jax.ShapeDtypeStruct((HEADS, 256, 512), bf16),
            jax.ShapeDtypeStruct((HEADS, 256, 256), bf16),
            jax.ShapeDtypeStruct((HEADS, 1792, 128), bf16),
            jax.ShapeDtypeStruct((HEADS, HALF, 128), bf16),
            jax.ShapeDtypeStruct((HEADS, HALF, 128), bf16),
            jax.ShapeDtypeStruct((FF, DP), bf16),
            jax.ShapeDtypeStruct((HALF, D), bf16),
            jax.ShapeDtypeStruct((HALF, DP), f32),
            jax.ShapeDtypeStruct((HALF, DP), bf16),
            jax.ShapeDtypeStruct((2, 2 * D, D), bf16),
            jax.ShapeDtypeStruct((2, 2 * D, D), f32),
            jax.ShapeDtypeStruct((NVEC, DP), f32),
            jax.ShapeDtypeStruct((8, FF), f32),
        ),
        in_specs=[SMEM, VMEM, ANY, VMEM, VMEM, VMEM, VMEM, VMEM, VMEM, VMEM, ANY, ANY],
        out_specs=(VMEM,) * 14,
        scratch_shapes=[
            pltpu.VMEM((HALF, DP), f32),
            pltpu.VMEM((SEQ, D), bf16),
            pltpu.VMEM((FF, DP), bf16),
            pltpu.VMEM((FF, DP), bf16),
            pltpu.VMEM((HALF, FF), bf16),
            pltpu.VMEM((HALF, FF), bf16),
            pltpu.VMEM((HALF, DP), bf16),
            pltpu.VMEM((HALF, DP), bf16),
            pltpu.VMEM((FF, D), f32),
            pltpu.SemaphoreType.DMA((5,)),
        ],
        compiler_params=pltpu.CompilerParams(vmem_limit_bytes=60 * 2**20),
        cost_estimate=pl.CostEstimate(
            flops=20 * 10**9, bytes_accessed=30 * 10**6, transcendentals=6 * 10**6
        ),
        name="forward_block",
    )(meta, attend, first, vec, bias_qv, bias_one, *weights, cot_own, cot_oth)


def backward_kernel(
    meta,
    attend,
    prob_a,
    prob_b,
    prob_c,
    keys_in,
    query_in,
    heads_in,
    table,
    branch,
    grad_attend,
    grads_send,
    grads_keep,
    bias_rows,
    mixed,
    grad_heads,
    grad_query,
    grad_scores,
    grads,
):
    core, clips = layout_of(meta)
    part = meta[0]
    pieces = own_pieces(core, clips)
    low_lane = lax.broadcasted_iota(jnp.int32, (1, 128), 1) < HD
    mixed[...] = jnp.zeros_like(mixed)

    def head(h, carry):
        base = mult(h * 4 * HD, 4 * HD)
        grad_out = dot(branch[...], table[pl.ds(base + 128, 128), :], NT)
        grad_out = jnp.where(low_lane, 0.0, grad_out).astype(bf16)
        grad_heads[...] = grad_out
        out = heads_in[h]
        inner = jnp.sum(grad_out.astype(f32) * out.astype(f32), axis=-1, keepdims=True)
        value_rows = jnp.sum(grad_out.astype(f32), axis=0, keepdims=True)
        for (q_at, q_rows, k_at, k_rows), prob in zip(SEGMENTS, (prob_a, prob_b, prob_c)):
            keys = keys_in[h, k_at : k_at + k_rows]
            step = min(q_rows, 256)
            for at in range(0, q_rows, step):
                rows = slice(q_at + at, q_at + at + step)
                grad_probs = dot(grad_heads[rows, :], keys, NT)
                probs = prob[h, at : at + step].astype(f32)
                scores = (probs * (grad_probs - inner[rows])).astype(bf16)
                grad_scores[at : at + step, 0:k_rows] = scores
                grad_query[rows, :] = dot(scores, keys, NN)
            both = dot(query_in[h, q_at : q_at + q_rows], grad_scores[0:q_rows, 0:k_rows], TN)
            both = both + dot(grad_heads[q_at : q_at + q_rows, :], prob[h], TN)
            both = both.astype(bf16)
            if k_at == 1536:
                lanes = pl.ds(mult(1536 + core * 256, 256), 256)
            else:
                lanes = slice(k_at, k_at + k_rows)
            mixed[pl.ds(base + HD, 128), lanes] = both
        queries = jnp.where(low_lane, grad_query[...] * 0.125, 0.0)
        bias_rows[h] = jnp.sum(queries.astype(bf16).astype(f32), axis=0, keepdims=True) + value_rows
        turned = jnp.transpose(queries)[0:HD].astype(bf16)
        for count, at, canon, _ in pieces:
            mixed[pl.ds(base, HD), pl.ds(mult(canon, 256), count)] = turned[:, at : at + count]
        out_rows = dot(out, branch[...], TN)
        grads[pl.ds(base + 3 * HD, HD), :] = out_rows[HD:, 0:D]
        return carry

    lax.fori_loop(0, HEADS, head, 0)
    grad_attend[...] = dot(mixed[...], table[...], TN).astype(bf16)
    for h in range(HEADS):
        rows = slice(h * 4 * HD, h * 4 * HD + 3 * HD)
        grads[rows, :] = dot(mixed[rows, :], attend[...], NN)[:, 0:D]
    for q in range(4):
        value = grads[pl.ds(mult(jnp.bitwise_xor(part, q) * D, 64), D), :]
        if q % 2:
            grads_send[q // 2] = value.astype(bf16)
        else:
            grads_keep[q // 2] = value


def backward_block(meta, attend, probs, keys, query, heads, table, branch):
    return pl.pallas_call(
        backward_kernel,
        out_shape=(
            jax.ShapeDtypeStruct((SEQ, DP), bf16),
            jax.ShapeDtypeStruct((2, D, D), bf16),
            jax.ShapeDtypeStruct((2, D, D), f32),
            jax.ShapeDtypeStruct((HEADS, 1, 128), f32),
        ),
        in_specs=[SMEM] + [VMEM] * 9,
        out_specs=(VMEM,) * 4,
        scratch_shapes=[
            pltpu.VMEM((FF, SEQ), bf16),
            pltpu.VMEM((HALF, 128), bf16),
            pltpu.VMEM((HALF, 128), f32),
            pltpu.VMEM((512, 1024), bf16),
            pltpu.VMEM((FF, D), f32),
        ],
        compiler_params=pltpu.CompilerParams(vmem_limit_bytes=56 * 2**20),
        cost_estimate=pl.CostEstimate(
            flops=15 * 10**9, bytes_accessed=20 * 10**6, transcendentals=0
        ),
        name="backward_block",
    )(meta, attend, *probs, keys, query, heads, table, branch)


def conv_back_kernel(
    meta,
    own,
    other,
    second_own,
    second_oth,
    first,
    x_own,
    vec,
    rows_in,
    out_own,
    out_oth,
    input_grad,
    block_out,
    rows_out,
    x0,
    xm,
    xp,
    xw,
    vb,
    sem,
):
    core, clips = layout_of(meta)
    small_core = (jnp.int32(0), jnp.int32(1))
    clear_gaps(x0, xm, xp)
    tap_rows(vec, vb)
    rows_out[...] = rows_in[...]

    for i in range(4):
        for b in range(SIZES[i] // 256):
            place = clips[i][0] + b * 256
            if i == 0:
                owner, at = b // 2, (b % 2) * 256
            elif i == 1:
                owner, at = b, 512
            else:
                owner, at = i - 2, 768
            mine = lax.div(place, HALF) == core
            row = mult(lax.rem(place, HALF), 256)

            @pl.when(mine & (core == owner))
            def _(row=row, at=at):
                block_out[pl.ds(row, 256), :] = out_own[at : at + 256, :]

            @pl.when(mine & (core != owner))
            def _(row=row, at=at):
                block_out[pl.ds(row, 256), :] = out_oth[at : at + 256, :]

    xw[2, :, :, 64:128] = jnp.zeros((HALF // 8, 8, 64), f32)
    for c in range(3):
        value = x_own[:, c * 128 : c * 128 + WIDTHS[c]].astype(f32)
        xw[c, :, :, 0 : WIDTHS[c]] = value.reshape(HALF // 8, 8, WIDTHS[c])

    mask = lax.broadcasted_iota(jnp.int32, (1, DP), 1) < D
    for i in range(4):
        for b in range(SIZES[i] // 256):
            place = clips[i][0] + b * 256
            if i == 0:
                owner, at = b // 2, (b % 2) * 256
            elif i == 1:
                owner, at = b, 512
            else:
                owner, at = i - 2, 768
            rows = slice(CANON[i] + b * 256, CANON[i] + b * 256 + 256)
            grad = own[rows, :].astype(f32) + other[rows, :].astype(f32)
            normed, scale = norm_parts(first[rows, :], mask)
            second = jnp.where(
                core == owner,
                second_own[at : at + 256, :],
                second_oth[at : at + 256, :].astype(f32),
            )
            whole = second + norm_back(grad, normed, scale, vec[28:29, :])
            whole = jnp.where(mask, whole, 0.0)
            for c in range(3):
                lanes = slice(c * 128, c * 128 + WIDTHS[c])
                put_shifted(x0, xm, xp, c, PTILES[i] + b * 32, whole[:, lanes], clips[i][2])

            @pl.when(lax.div(place, HALF) == core)
            def _(grad=grad, normed=normed, whole=whole):
                rows_out[27:28, :] += jnp.sum(whole, axis=0, keepdims=True)
                rows_out[28:29, :] += jnp.sum(grad * normed, axis=0, keepdims=True)
                rows_out[29:30, :] += jnp.sum(grad, axis=0, keepdims=True)

    at_tile = lax.broadcasted_iota(jnp.int32, (2, 8, 128), 0)
    blocks = []
    for b in range(4):
        place = core * HALF + b * 256
        index = jnp.int32(0)
        for i in range(4):
            begin = clips[i][0]
            index = jnp.where((place >= begin) & (place < begin + SIZES[i]), i, index)
        pick = lambda values, index=index: jnp.where(
            index == 0,
            values[0],
            jnp.where(index == 1, values[1], jnp.where(index == 2, values[2], values[3])),
        )
        width = lax.div(pick([c[2] for c in clips]), 8)
        plane = pick([c[1] for c in clips]) * width
        local = lax.div(place - pick([c[0] for c in clips]), 8)
        tile = local + pick([jnp.int32(p) for p in PTILES])
        blocks.append((width, plane, local, tile))

    for c in range(3):
        sums = tuple(jnp.zeros((8, 128), f32) for _ in range(27))
        for b, (width, plane, local, tile) in enumerate(blocks):

            def step(n, sums, b=b, c=c, width=width, plane=plane, local=local, tile=tile):
                sums = list(sums)
                place = (at_tile + (local + n * 2)) & (plane - 1)
                inside = (place >= width, None, place < plane - width)
                x = xw[c, pl.ds(b * 32 + n * 2, 2)]
                at0 = tile + n * 2
                total = x0[c, pl.ds(at0, 2)]
                for dr in range(3):
                    x_here = x if dr == 1 else jnp.where(inside[dr], x, 0.0)
                    piece = None
                    for df in range(3):
                        at = pl.ds(at0 + (df - 1) * plane + (dr - 1) * width, 2)
                        for dc, ref in enumerate((xm, x0, xp)):
                            k = 26 - (9 * df + 3 * dr + dc)
                            value = ref[c, at]
                            term = value * vb[k, c]
                            piece = term if piece is None else piece + term
                            product = value * x_here
                            sums[k] = sums[k] + (product[0] + product[1])
                    if dr != 1:
                        piece = jnp.where(inside[dr], piece, 0.0)
                    total = total + piece
                rows = pl.ds(mult(b * 256 + n * 16, 16), 16)
                lanes = slice(c * 128, c * 128 + WIDTHS[c])
                input_grad[rows, lanes] = total.reshape(16, 128)[:, 0 : WIDTHS[c]].astype(bf16)
                return tuple(sums)

            sums = lax.fori_loop(0, 16, step, sums)
        for k in range(27):
            lanes = slice(c * 128, c * 128 + 128)
            rows_out[k : k + 1, lanes] = jnp.sum(sums[k], axis=0, keepdims=True)


def conv_backward(meta, own, other, second_own, second_oth, first, x_own, vec, rows, outs):
    return pl.pallas_call(
        conv_back_kernel,
        out_shape=(
            jax.ShapeDtypeStruct((HALF, D), bf16),
            jax.ShapeDtypeStruct((HALF, D), bf16),
            jax.ShapeDtypeStruct((NVEC, DP), f32),
        ),
        in_specs=[SMEM] + [VMEM] * 10,
        out_specs=(VMEM,) * 3,
        scratch_shapes=[
            pltpu.VMEM((3, ALL_TILES, 8, 128), f32),
            pltpu.VMEM((3, ALL_TILES, 8, 128), f32),
            pltpu.VMEM((3, ALL_TILES, 8, 128), f32),
            pltpu.VMEM((3, HALF // 8, 8, 128), f32),
            pltpu.VMEM((27, 3, 8, 128), f32),
            pltpu.SemaphoreType.DMA((2,)),
        ],
        compiler_params=pltpu.CompilerParams(vmem_limit_bytes=48 * 2**20),
        cost_estimate=pl.CostEstimate(
            flops=4 * 10**9, bytes_accessed=14 * 10**6, transcendentals=0
        ),
        name="conv_backward",
    )(meta, own, other, second_own, second_oth, first, x_own, vec, rows, *outs)


def spread_kernel(first_tile, meta, keep, recv, out_send, out_keep, slots):
    half = SLOTS // 2
    slots[...] = jnp.zeros_like(slots)

    def move(j, carry):
        rows = pl.ds(mult(j * TR, TR), TR)
        value = keep[rows, :] + recv[rows, :].astype(f32)
        slots[meta[META_TILES + first_tile + j]] = value
        return carry

    lax.fori_loop(0, keep.shape[0] // TR, move, 0)
    out_keep[...] = slots[0:half]
    out_send[...] = slots[half:].astype(bf16)


def spread(first_tile, meta, keep, recv):
    half = SLOTS // 2
    return pl.pallas_call(
        functools.partial(spread_kernel, first_tile),
        out_shape=(
            jax.ShapeDtypeStruct((half, TR, D), bf16),
            jax.ShapeDtypeStruct((half, TR, D), f32),
        ),
        in_specs=[SMEM, VMEM, VMEM],
        out_specs=(VMEM, VMEM),
        scratch_shapes=[pltpu.VMEM((SLOTS, TR, D), f32)],
        name="spread_tiles",
    )(meta, keep, recv)


def soap_kernel(corr, grad_a, grad_b, masters, left, right, first, second, out_w, out_m, out_v):
    highest = lax.Precision.HIGHEST

    def full(a, b, dims):
        return lax.dot_general(a, b, dims, precision=highest, preferred_element_type=f32)

    for s in range(masters.shape[0]):
        basis = left[s]
        rotated = full(basis, grad_a[s] + grad_b[s], TN)
        rotated = full(rotated, right[s], NN)
        new_first = beta_one * first[s] + (1.0 - beta_one) * rotated
        new_second = beta_two * second[s] + (1.0 - beta_two) * rotated * rotated
        out_m[s] = new_first
        out_v[s] = new_second
        direction = new_first / corr[0] / (jnp.sqrt(new_second / corr[1]) + adam_eps)
        back = full(full(basis, direction, NN), right[s], NT)
        out_w[s] = masters[s] - matrix_rate * (back + matrix_decay * masters[s])


def soap(corr, grad_a, grad_b, masters, left, right, first, second):
    shape = jax.ShapeDtypeStruct(masters.shape, f32)
    return pl.pallas_call(
        soap_kernel,
        out_shape=(shape, shape, shape),
        in_specs=[SMEM] + [VMEM] * 7,
        out_specs=(VMEM,) * 3,
        compiler_params=pltpu.CompilerParams(vmem_limit_bytes=24 * 2**20),
        cost_estimate=pl.CostEstimate(
            flops=2 * 10**9, bytes_accessed=6 * 10**6, transcendentals=0
        ),
        name="tile_update",
    )(corr, grad_a, grad_b, masters, left, right, first, second)


def flipped(value, axis, bit):
    size = lax.axis_size(axis)
    return lax.ppermute(value, axis, [(i, i ^ bit) for i in range(size)])


def reduce_slots(send, keep, bits):
    for n, bit in enumerate(bits):
        total = keep + flipped(send, "dp", bit).astype(f32)
        if n + 1 < len(bits):
            half = total.shape[0] // 2
            keep, send = total[:half], total[half:].astype(bf16)
    return total


def on_device(
    block_input,
    cotangent,
    clip_starts,
    clip_shapes,
    tile_slot,
    masters,
    left_bases,
    right_bases,
    first_moment,
    second_moment,
    vectors,
    vector_first,
    vector_second,
    step_count,
):
    part = lax.axis_index("tp")
    rank = lax.axis_index("dp")
    bits = [1 << n for n in range(lax.axis_size("dp").bit_length() - 1)]
    owned = masters.shape[1]

    relative = jnp.bitwise_xor(tile_slot // owned, rank)
    position = sum(
        ((relative >> n) & 1) << (len(bits) - 1 - n) for n in range(len(bits))
    ) * owned + tile_slot % owned
    meta = jnp.concatenate(
        [part[None].astype(jnp.int32), clip_starts.reshape(-1), clip_shapes.reshape(-1), position]
    )
    vec = jnp.pad(vectors, ((0, 0), (0, DP - D)))
    vec = vec.at[29, D].set(1.0).at[34, D].set(1.0)
    bias_qv = jnp.concatenate(
        [vectors[30].reshape(HEADS, 1, HD), vectors[31].reshape(HEADS, 1, HD)], axis=2
    )
    bias_one = vectors[35:39].reshape(1, FF)

    x_oth = flipped(block_input, "tp", 1)
    cot_oth = flipped(cotangent, "tp", 1)
    held = masters[0].astype(bf16)
    for bit in reversed(bits):
        held = jnp.concatenate([held, flipped(held, "dp", bit)], axis=0)
    held_core = flipped(held, "tp", 1)
    held_far = flipped(held, "tp", 2)
    held_both = flipped(held_far, "tp", 1)

    attend, first = conv_forward(meta, block_input, x_oth, vec)
    (
        prob_a,
        prob_b,
        prob_c,
        keys,
        query,
        heads,
        table,
        block_out,
        grad_second,
        branch,
        fc_send,
        fc_keep,
        rows_mlp,
        fc_rows,
    ) = forward_block(
        meta,
        attend,
        first,
        vec,
        bias_qv,
        bias_one,
        (held, held_core, held_far, held_both),
        cotangent,
        cot_oth,
    )
    block_oth = flipped(block_out, "tp", 1)
    branch_oth = flipped(branch, "tp", 1)

    def over_tp(send, keep):
        total = keep + flipped(send, "tp", 1).astype(f32)
        return total[0], flipped(total[1].astype(bf16), "tp", 2)

    fc_total = reduce_slots(*spread(D // TR, meta, *over_tp(fc_send, fc_keep)), bits)

    grad_attend, table_send, table_keep, bias_rows = backward_block(
        meta, attend, (prob_a, prob_b, prob_c), keys, query, heads, table, branch
    )
    grad_attend_oth = flipped(grad_attend, "tp", 1)
    table_total = reduce_slots(*spread(0, meta, *over_tp(table_send, table_keep)), bits)

    rows = jnp.concatenate(
        [
            rows_mlp[:30, :D],
            bias_rows[:, 0, :HD].reshape(1, D),
            bias_rows[:, 0, HD:].reshape(1, D),
            rows_mlp[32:35, :D],
            fc_rows[0].reshape(GROUPS, D),
            rows_mlp[39:, :D],
        ],
        axis=0,
    )
    rows = jnp.pad(rows, ((0, 0), (0, DP - D)))
    input_grad, block_output, vector_grad = conv_backward(
        meta,
        grad_attend,
        grad_attend_oth,
        grad_second,
        branch_oth,
        first,
        block_input,
        vec,
        rows,
        (block_out, block_oth),
    )
    for axis, flips in (("tp", (1, 2)), ("dp", bits)):
        for bit in flips:
            vector_grad = vector_grad + flipped(vector_grad, axis, bit)
    vector_grad = vector_grad[:, :D]

    steps = step_count[0].astype(f32)
    corr_one = 1.0 - jnp.power(beta_one, steps)
    corr_two = 1.0 - jnp.power(beta_two, steps)
    new_masters, new_first, new_second = soap(
        jnp.stack([corr_one, corr_two]),
        fc_total,
        table_total,
        masters[0],
        left_bases[0],
        right_bases[0],
        first_moment[0],
        second_moment[0],
    )
    new_vector_first = beta_one * vector_first + (1.0 - beta_one) * vector_grad
    new_vector_second = beta_two * vector_second + (1.0 - beta_two) * vector_grad * vector_grad
    direction = new_vector_first / corr_one
    direction = direction / (jnp.sqrt(new_vector_second / corr_two) + adam_eps)
    return (
        block_output,
        input_grad,
        new_masters[None],
        new_first[None],
        new_second[None],
        vectors - vector_rate * direction,
        new_vector_first,
        new_vector_second,
    )


def solution(mesh):
    tokens = P(("dp", "tp"), None)
    tiles = P("tp", "dp", None, None)
    in_specs = (
        tokens,
        tokens,
        P("dp", None),
        P("dp", None, None),
        P(),
        tiles,
        tiles,
        tiles,
        tiles,
        tiles,
        P(),
        P(),
        P(),
        P(),
    )
    out_specs = (tokens, tokens, tiles, tiles, tiles, P(), P(), P())
    return jax.shard_map(
        on_device, mesh=mesh, in_specs=in_specs, out_specs=out_specs, check_vma=False
    )
```

```python
import functools

import jax
import jax.numpy as jnp
from jax import lax
from jax.experimental import pallas as pl
from jax.experimental.pallas import tpu as pltpu
from jax.sharding import PartitionSpec as P

D = 320
DP = 384
HEADS = 5
HD = 64
FF = 1280
SEQ = 2048
HALF = SEQ // 2
TR = 16
SLOTS = 64
TILES = 60
NVEC = 40
GROUPS = FF // D

norm_eps = 1e-06
beta_one = 0.9
beta_two = 0.99
adam_eps = 1e-08
matrix_rate = 0.1
matrix_decay = 0.05
vector_rate = 0.5

SIZES = (1024, 512, 256, 256)
CANON = (0, 1024, 1536, 1792)
GAP = 34
PTILES = (GAP, 2 * GAP + 128, 3 * GAP + 192, 4 * GAP + 224)
ALL_TILES = 5 * GAP + 256
WIDTHS = (128, 128, 64)

f32 = jnp.float32
bf16 = jnp.bfloat16
NN = (((1,), (0,)), ((), ()))
NT = (((1,), (1,)), ((), ()))
TN = (((0,), (0,)), ((), ()))
TT = (((0,), (1,)), ((), ()))

SMEM = pl.BlockSpec(memory_space=pltpu.SMEM)
VMEM = pl.BlockSpec(memory_space=pltpu.VMEM)
ANY = pl.BlockSpec(memory_space=pltpu.HBM)
LOOSE = pl.BlockSpec(memory_space=pl.ANY)


def dot(a, b, dims):
    return lax.dot_general(a, b, dims, preferred_element_type=f32)


def cost(microseconds):
    return pl.CostEstimate(flops=0, bytes_accessed=int(microseconds * 3.5e6), transcendentals=0)


def mult(value, step):
    return pl.multiple_of(value, step)


META_STARTS = 1
META_SHAPES = 9
META_TILES = 33


def layout_of(meta):
    part = meta[0]
    core = lax.rem(part, 2)
    row = lax.div(part, 2)
    starts = [meta[META_STARTS + row * 4 + i] for i in range(4)]
    shapes = [[meta[META_SHAPES + row * 12 + 3 * i + k] for k in range(3)] for i in range(4)]
    counts = [s[0] * s[1] * s[2] for s in shapes]
    seen = jnp.int32(0)
    marks = [[], [], [], []]
    for i in range(4):
        small = (counts[i] == 256).astype(jnp.int32)
        marks[0].append((counts[i] == 1024).astype(jnp.int32))
        marks[1].append((counts[i] == 512).astype(jnp.int32))
        marks[2].append(small * (1 - seen))
        marks[3].append(small * seen)
        seen = jnp.maximum(seen, small)
    clips = []
    for mark in marks:
        pick = lambda values: sum(m * v for m, v in zip(mark, values))
        clips.append((pick(starts), pick([s[1] for s in shapes]), pick([s[2] for s in shapes])))
    return core, clips


def own_pieces(core, clips):
    small_start = jnp.where(core == 0, clips[2][0], clips[3][0])
    return (
        (512, 0, core * 512, clips[0][0] + core * 512),
        (256, 512, 1024 + core * 256, clips[1][0] + core * 256),
        (256, 768, 1536 + core * 256, small_start),
    )


def identity(rows, columns):
    at = [lax.broadcasted_iota(jnp.int32, (rows, columns), n) for n in range(2)]
    return jnp.where(at[0] == at[1], 1.0, 0.0).astype(bf16)


def clear_gaps(padded):
    for at in (0,) + tuple(p + s // 8 for p, s in zip(PTILES, SIZES)):
        padded[:, at : at + GAP] = jnp.zeros((3, GAP, 8, 128), f32)


def put_rows(padded, tile, value):
    for c, width in enumerate(WIDTHS):
        piece = value[:, c * 128 : c * 128 + width].reshape(32, 8, width)
        padded[c, pl.ds(tile, 32), :, 0:width] = piece


def tap_rows(vec, vb):
    for k in range(27):
        for c in range(3):
            vb[k, c] = jnp.broadcast_to(vec[k : k + 1, c * 128 : c * 128 + 128], (8, 128))


def block_of(clips, place):
    index = jnp.int32(0)
    for i in range(4):
        begin = clips[i][0]
        index = jnp.where((place >= begin) & (place < begin + SIZES[i]), i, index)

    def pick(values):
        high = jnp.where(index == 2, values[2], values[3])
        return jnp.where(index == 0, values[0], jnp.where(index == 1, values[1], high))

    width = lax.div(pick([c[2] for c in clips]), 8)
    plane = pick([c[1] for c in clips]) * width
    local = lax.div(place - pick([c[0] for c in clips]), 8)
    return width, plane, local, local + pick([jnp.int32(p) for p in PTILES])


def neighbours(padded, c, tile, tiles, width, plane, local):
    place = (lax.broadcasted_iota(jnp.int32, (tiles, 8, 128), 0) + local) & (plane - 1)
    inside = (place >= width, None, place < plane - width)
    for df in range(3):
        for dr in range(3):
            value = padded[c, pl.ds(tile + (df - 1) * plane + (dr - 1) * width, tiles)]
            yield 9 * df + 3 * dr, value if dr == 1 else jnp.where(inside[dr], value, 0.0)


def columns(tiles, width):
    at = lax.broadcasted_iota(jnp.int32, (tiles * 8, 128), 0) & (width * 8 - 1)
    return at != width * 8 - 1, at != 0


def to_left(value, not_first):
    tiles = value.shape[0]
    rolled = pltpu.roll(value.reshape(tiles * 8, 128), 1, 0)
    return jnp.where(not_first, rolled, 0.0).reshape(tiles, 8, 128)


def to_right(value, not_last):
    tiles = value.shape[0]
    rolled = pltpu.roll(value.reshape(tiles * 8, 128), tiles * 8 - 1, 0)
    return jnp.where(not_last, rolled, 0.0).reshape(tiles, 8, 128)


UNIT = 8


def conv_kernel(
    meta, x_own, x_oth, vec, after, attend_out, first_out, padded, vb, first, attend, sem
):
    core, clips = layout_of(meta)
    clear_gaps(padded)
    tap_rows(vec, vb)
    turn = identity(256, 256)
    for half, ref in ((core, x_own), (1 - core, x_oth)):
        for b in range(4):
            tile = block_of(clips, half * HALF + b * 256)[3]
            put_rows(padded, tile, dot(turn, ref[:, b * 256 : b * 256 + 256], NT))
    copies = []
    mask = lax.broadcasted_iota(jnp.int32, (1, DP), 1) < D
    for i in range(4):
        width = lax.div(clips[i][2], 8)
        plane = clips[i][1] * width

        def unit(u, carry, i=i, width=width, plane=plane):
            tile = u * UNIT + PTILES[i]
            not_last, not_first = columns(UNIT, width)
            rows = pl.ds(mult(u * (8 * UNIT) + CANON[i], 8 * UNIT), 8 * UNIT)
            for c in range(3):
                sums = [None] * 3
                for k, value in neighbours(padded, c, tile, UNIT, width, plane, u * UNIT):
                    for dc in range(3):
                        term = value * vb[k + dc, c]
                        sums[dc] = term if sums[dc] is None else sums[dc] + term
                total = padded[c, pl.ds(tile, UNIT)] + vec[27:28, c * 128 : c * 128 + 128]
                total = total + sums[1]
                total = total + to_left(sums[0], not_first)
                total = total + to_right(sums[2], not_last)
                first[rows, c * 128 : c * 128 + 128] = total.reshape(8 * UNIT, 128)
            return carry

        lax.fori_loop(0, SIZES[i] // (8 * UNIT), unit, 0)
        rows = pl.ds(CANON[i], SIZES[i])
        copies.append(pltpu.make_async_copy(first.at[rows], first_out.at[rows], sem.at[0, i]))
        copies[-1].start()

        def norm(n, carry, i=i):
            rows = pl.ds(mult(CANON[i] + n * 256, 256), 256)
            normed, _ = norm_parts(first[rows, :], mask)
            attend[rows, :] = (normed * vec[28:29, :] + vec[29:30, :]).astype(bf16)
            return carry

        lax.fori_loop(0, SIZES[i] // 256, norm, 0)
        copies.append(pltpu.make_async_copy(attend.at[rows], attend_out.at[rows], sem.at[1, i]))
        copies[-1].start()
    for copy in copies:
        copy.wait()


def conv_forward(meta, x_own, x_oth, vec, after):
    return pl.pallas_call(
        conv_kernel,
        out_shape=(
            jax.ShapeDtypeStruct((SEQ, DP), bf16),
            jax.ShapeDtypeStruct((SEQ, DP), f32),
        ),
        in_specs=[SMEM, VMEM, VMEM, VMEM, ANY],
        out_specs=(ANY, ANY),
        scratch_shapes=[
            pltpu.VMEM((3, ALL_TILES, 8, 128), f32),
            pltpu.VMEM((27, 3, 8, 128), f32),
            pltpu.VMEM((SEQ, DP), f32),
            pltpu.VMEM((SEQ, DP), bf16),
            pltpu.SemaphoreType.DMA((2, 4)),
        ],
        compiler_params=pltpu.CompilerParams(vmem_limit_bytes=58 * 2**20),
        cost_estimate=cost(12),
        name="conv_forward",
    )(meta, x_own, x_oth, vec, after)


def two_parts(value):
    high = value.astype(bf16)
    return high, (value - high.astype(f32)).astype(bf16)


def norm_parts(values, mask):
    values = jnp.where(mask, values, 0.0)
    mean = jnp.sum(values, axis=-1, keepdims=True) * (1.0 / D)
    center = jnp.where(mask, values - mean, 0.0)
    scale = lax.rsqrt(jnp.sum(center * center, axis=-1, keepdims=True) * (1.0 / D) + norm_eps)
    return center * scale, scale


def norm_back(grad, normed, scale, gain):
    scaled = grad * gain
    mean = jnp.sum(scaled, axis=-1, keepdims=True) * (1.0 / D)
    inner = jnp.sum(scaled * normed, axis=-1, keepdims=True) * (1.0 / D)
    return scale * (scaled - mean - normed * inner)


def phi_parts(v):
    density = jnp.exp(v * v * -0.5) * 0.3989422804014327
    base = 1.0 + 0.2316419 * jnp.abs(v)
    t = pl.reciprocal(base, approx=True)
    t = t * (2.0 - base * t)
    poly = 1.330274429
    for factor in (-1.821255978, 1.781477937, -0.356563782, 0.319381530):
        poly = poly * t + factor
    upper = density * (poly * t)
    return jnp.where(v >= 0.0, 1.0 - upper, upper), density


SEGMENTS = ((0, 512, 0, 1024), (512, 256, 1024, 512), (768, 256, 1536, 256))
PROBS = ((1024, 512), (512, 256), (256, 256))
HEAD_LANES = HEADS * 128


def table_place(run):
    head, kind = divmod(run, 4)
    return (1, 0, 0, 1)[kind], head * 128 + (0, 0, 64, 64)[kind]


def forward_kernel(places_of, *refs):
    meta, attend_ref, first, vec, bias_qv, bias_one, cot_own, cot_oth = refs[:8]
    held = refs[8 : 8 + len(places_of)]
    refs = refs[8 + len(places_of) :]
    prob_refs, keys_ref, query_ref, heads_ref = refs[:3], refs[3], refs[4], refs[5]
    table_ref, block_ref, branch_ref, send_ref, keep_ref, rows_out, fc_rows = refs[6:13]
    (
        prob_a,
        prob_b,
        prob_c,
        keys,
        query,
        heads,
        table,
        block_out,
        branch,
        grads,
        wide,
        pres,
        backs,
        second,
        tiles,
        fc_one,
        fc_two,
        hidden,
        grad_pre,
        mlp_in,
        cot_low,
        attend,
        keys_turned,
        sem,
        prob_sem,
        out_sem,
    ) = refs[13:]
    core, clips = layout_of(meta)
    part = meta[0]
    pieces = own_pieces(core, clips)
    copies = []
    for ref, (low, entries) in zip(held, places_of):
        count, owned = ref.shape[1:3]
        for n, (group, side) in enumerate(entries):
            into = tiles.at[group, pl.ds(side * count, count), pl.ds(low, owned)]
            copies.append(pltpu.make_async_copy(ref.at[n], into, sem.at[len(copies)]))
    for count, at, canon, _ in pieces:
        copies.append(
            pltpu.make_async_copy(
                first.at[pl.ds(mult(canon, 256), count)],
                second.at[pl.ds(at, count)],
                sem.at[len(copies)],
            )
        )
    copies.append(pltpu.make_async_copy(attend_ref, attend, sem.at[len(copies)]))
    for copy in copies:
        copy.start()
    outs = []

    def send_out(source, target):
        outs.append(pltpu.make_async_copy(source, target, out_sem.at[len(outs)]))
        outs[-1].start()

    turn = identity(256, 256)
    cot_low[:, 256:DP] = jnp.zeros((HALF, 128), bf16)
    for n in range(4):
        place = (pieces[0][3], pieces[0][3] + 256, pieces[1][3], pieces[2][3])[n]
        lanes = pl.ds(mult(lax.rem(place, HALF), 256), 256)
        mine = lax.div(place, HALF) == core
        for ref, here in ((cot_own, mine), (cot_oth, jnp.logical_not(mine))):

            @pl.when(here)
            def _(ref=ref, n=n, lanes=lanes):
                value = dot(turn, ref[:, lanes], NT).astype(bf16)
                cot_low[n * 256 : n * 256 + 256, 0:D] = value

    table[:, :, 256:DP] = jnp.zeros((2, HEAD_LANES, 128), bf16)
    for ref in (fc_one, fc_two):
        ref[:, 256:DP] = jnp.zeros((FF, 128), bf16)
    rows_out[...] = jnp.zeros_like(rows_out)
    fc_rows[...] = jnp.zeros_like(fc_rows)
    for copy in copies:
        copy.wait()
    owned = tiles.shape[2]

    def tile_of(group, tile):
        slot = meta[META_TILES + tile]
        at = jnp.bitwise_xor(part, group)
        return tiles[at, lax.div(slot, owned), lax.rem(slot, owned)]

    for g in range(GROUPS):
        for j in range(D // TR):
            side, row = table_place(g * 5 + j // 4)
            row = row + j % 4 * TR
            table[side, row : row + TR, 0:D] = tile_of(g, j)
    send_out(table, table_ref)

    mask = lax.broadcasted_iota(jnp.int32, (1, DP), 1) < D
    low_lanes = (lax.broadcasted_iota(jnp.int32, (1, HEAD_LANES), 1) & 127) < HD
    low_lane = low_lanes[:, 0:128]
    bias_q = jnp.where(low_lanes, bias_qv[...], 0.0)
    bias_v = bias_qv[...] - bias_q
    small_rows = pl.ds(mult(1536 + core * 256, 256), 256)
    for at in range(0, 1536, 512):
        value = dot(attend[at : at + 512, :], table[0], NT) + bias_v
        keys[at : at + 512, :] = value.astype(bf16)
    keys[1536:1792, :] = (dot(attend[small_rows, :], table[0], NT) + bias_v).astype(bf16)
    for count, at, canon, _ in pieces:
        value = dot(attend[pl.ds(mult(canon, 256), count), :], table[1], NT) + bias_q
        query[at : at + count, :] = jnp.where(low_lanes, value, 0.0).astype(bf16) * bf16(0.125)
    send_out(keys, keys_ref)
    send_out(query, query_ref)
    small_turn = identity(128, 128)
    for h in range(HEADS):
        lanes = slice(h * 128, h * 128 + 128)
        keys_turned[lanes, :] = dot(small_turn, keys[:, lanes], NT).astype(bf16)

    probs = (prob_a, prob_b, prob_c)

    def prob_copies(h):
        return [
            pltpu.make_async_copy(buf.at[h % 2], out.at[h], prob_sem.at[h % 2, n])
            for n, (buf, out) in enumerate(zip(probs, prob_refs))
        ]

    blocks = [
        (h, n, at)
        for h in range(HEADS)
        for n in range(3)
        for at in range(0, SEGMENTS[n][1], 256)
    ]

    def parts_of(block):
        h, n, at = block
        q_at, _, k_at, k_rows = SEGMENTS[n]
        lanes = slice(h * 128, h * 128 + 128)
        return slice(q_at + at, q_at + at + 256), slice(k_at, k_at + k_rows), lanes, k_rows

    def score_stage(index):
        rows, k_range, lanes, k_rows = parts_of(blocks[index])
        wide[index % 3, 0:k_rows] = dot(keys[k_range, lanes], query[rows, lanes], NT)

    def softmax_stage(index):
        h, n, at = blocks[index]
        k_rows = SEGMENTS[n][3]
        if h >= 2 and n == 0 and at == 0:
            for copy in prob_copies(h - 2):
                copy.wait()
        scores = wide.at[index % 3]
        peak = jnp.max(scores[0:k_rows], axis=0, keepdims=True)
        total = jnp.zeros((8, 256), f32)
        for r in range(0, k_rows, 32):
            weights = jnp.exp(scores[r : r + 32] - peak)
            scores[r : r + 32] = weights
            total = total + jnp.sum(weights.reshape(4, 8, 256), axis=0)
        inverse = 1.0 / jnp.sum(total, axis=0, keepdims=True)
        for r in range(0, k_rows, 32):
            value = (scores[r : r + 32] * inverse).astype(bf16)
            probs[n][h % 2, r : r + 32, at : at + 256] = value

    def value_stage(index):
        h, n, at = blocks[index]
        rows, k_range, lanes, _ = parts_of(blocks[index])
        out = dot(keys_turned[lanes, k_range], probs[n][h % 2, :, at : at + 256], NN)
        out = jnp.where(low_lane, 0.0, dot(turn, out.astype(bf16), NT))
        heads[rows, lanes] = out.astype(bf16)
        if index + 1 == len(blocks) or blocks[index + 1][0] != h:
            for copy in prob_copies(h):
                copy.start()

    score_stage(0)
    for index in range(len(blocks)):
        if index + 1 < len(blocks):
            score_stage(index + 1)
        if index:
            value_stage(index - 1)
        softmax_stage(index)
    value_stage(len(blocks) - 1)
    send_out(heads, heads_ref)
    for g in range(GROUPS):
        for kind, ref in ((1, fc_one), (2, fc_two)):
            for j in range(D // TR):
                row = g * D + j * TR
                ref[row : row + TR, 0:D] = tile_of(g, kind * 20 + j)

    for at in range(0, HALF, 256):
        rows = slice(at, at + 256)
        before = jnp.where(mask, second[rows, :] + vec[32:33, :], 0.0)
        second[rows, :] = before + dot(heads[rows, :], table[1], NN)

    kept = {}

    def norm_stage(n):
        rows = slice(n * 256, n * 256 + 256)
        normed, scale = norm_parts(second[rows, :], mask)
        mlp_in[rows, :] = (normed * vec[33:34, :] + vec[34:35, :]).astype(bf16)
        kept[n] = normed, scale

    def pre_stage(t):
        rows = slice(t // 5 * 256, t // 5 * 256 + 256)
        lanes = slice(t % 5 * 256, t % 5 * 256 + 256)
        pres[t % 3] = dot(mlp_in[rows, :], fc_one[lanes, :], NT)
        backs[t % 3] = dot(cot_low[rows, :], fc_two[lanes, :], NT)

    def gelu_stage(t):
        lanes = slice(t % 5 * 256, t % 5 * 256 + 256)
        total = jnp.zeros((8, 256), f32)
        for r in range(0, 256, 16):
            rows = slice(t // 5 * 256 + r, t // 5 * 256 + r + 16)
            pre = pres[t % 3, r : r + 16] + bias_one[:, lanes]
            below, density = phi_parts(pre)
            hidden[rows, lanes] = (pre * below).astype(bf16)
            back = backs[t % 3, r : r + 16] * (below + pre * density)
            back_low = back.astype(bf16)
            grad_pre[rows, lanes] = back_low
            back = back_low.astype(f32)
            total = total + (back[0:8] + back[8:16])
        fc_rows[:, lanes] += total

    def result_stage(n):
        rows = slice(n * 256, n * 256 + 256)
        normed, scale = kept.pop(n)
        cot_wide = cot_low[rows, :].astype(f32)
        result = second[rows, :] + dot(hidden[rows, :], fc_two[...], NN) + vec[39:40, :]
        block_out[rows, :] = result.astype(bf16)
        grad_in = dot(grad_pre[rows, :], fc_one[...], NN)
        rows_out[33:34, :] += jnp.sum(grad_in * normed, axis=0, keepdims=True)
        rows_out[34:35, :] += jnp.sum(grad_in, axis=0, keepdims=True)
        rows_out[39:40, :] += jnp.sum(cot_wide, axis=0, keepdims=True)
        whole = cot_wide + norm_back(grad_in, normed, scale, vec[33:34, :])
        low = jnp.where(mask, whole, 0.0).astype(bf16)
        branch[rows, :] = low
        rows_out[32:33, :] += jnp.sum(low.astype(f32), axis=0, keepdims=True)

    norm_stage(0)
    pre_stage(0)
    for t in range(20):
        if t + 1 < 20:
            if (t + 1) % 5 == 0:
                norm_stage((t + 1) // 5)
            pre_stage(t + 1)
        gelu_stage(t)
        if t % 5 == 0 and t:
            result_stage(t // 5 - 1)
    result_stage(3)
    send_out(branch, branch_ref)
    send_out(block_out, block_ref)
    for kind, (left, right) in enumerate(((grad_pre, mlp_in), (hidden, cot_low))):
        value = dot(left[...], right[...], TN)
        rows = slice(kind * D, kind * D + D)
        for g in range(GROUPS):
            at = jnp.bitwise_xor(part, g)
            piece = value[g * D : g * D + D].astype(bf16)
            grads[lax.rem(at, 2), lax.div(at, 2), rows] = piece
        rows = pl.ds(kind * D, D)
        send_out(grads.at[1, :, rows], send_ref.at[:, rows])
        send_out(grads.at[0, :, rows], keep_ref.at[:, rows])
    for copy in outs + prob_copies(HEADS - 2) + prob_copies(HEADS - 1):
        copy.wait()


def forward_block(
    meta, attend, first, vec, bias_qv, bias_one, cot_own, cot_oth, held, places_of, ranks
):
    owned = SLOTS // ranks
    probs = [(HEADS,) + shape for shape in PROBS]
    shapes = probs + [
        (1792, HEAD_LANES),
        (HALF, HEAD_LANES),
        (HALF, HEAD_LANES),
        (2, HEAD_LANES, DP),
        (HALF, DP),
        (HALF, DP),
        (2, 2 * D, DP),
        (2, 2 * D, DP),
    ]
    return pl.pallas_call(
        functools.partial(forward_kernel, places_of),
        out_shape=[jax.ShapeDtypeStruct(shape, bf16) for shape in shapes]
        + [jax.ShapeDtypeStruct((NVEC, DP), f32), jax.ShapeDtypeStruct((8, FF), f32)],
        in_specs=[SMEM, ANY, ANY, VMEM, VMEM, VMEM, VMEM, VMEM] + [LOOSE] * len(held),
        out_specs=[ANY] * 11 + [VMEM] * 2,
        scratch_shapes=[pltpu.VMEM((2,) + shape, bf16) for shape in PROBS]
        + [pltpu.VMEM(shape, bf16) for shape in shapes[3:9]]
        + [
            pltpu.VMEM((2, 2, 2 * D, DP), bf16),
            pltpu.VMEM((3, 1024, 256), f32),
            pltpu.VMEM((3, 256, 256), f32),
            pltpu.VMEM((3, 256, 256), f32),
            pltpu.VMEM((HALF, DP), f32),
            pltpu.VMEM((GROUPS, ranks, owned, TR, D), bf16),
            pltpu.VMEM((FF, DP), bf16),
            pltpu.VMEM((FF, DP), bf16),
            pltpu.VMEM((HALF, FF), bf16),
            pltpu.VMEM((HALF, FF), bf16),
            pltpu.VMEM((HALF, DP), bf16),
            pltpu.VMEM((HALF, DP), bf16),
            pltpu.VMEM((SEQ, DP), bf16),
            pltpu.VMEM((HEAD_LANES, 1792), bf16),
            pltpu.SemaphoreType.DMA((2 * len(held) + 4,)),
            pltpu.SemaphoreType.DMA((2, 3)),
            pltpu.SemaphoreType.DMA((10,)),
        ],
        compiler_params=pltpu.CompilerParams(vmem_limit_bytes=44 * 2**20),
        cost_estimate=cost(30),
        name="forward_block",
    )(meta, attend, first, vec, bias_qv, bias_one, cot_own, cot_oth, *held)


def backward_kernel(
    meta,
    attend_ref,
    prob_ra,
    prob_rb,
    prob_rc,
    keys_in,
    query_in,
    heads_in,
    table_ref,
    branch_ref,
    grad_attend,
    send_ref,
    keep_ref,
    bias_rows,
    prob_a,
    prob_b,
    prob_c,
    keys,
    query,
    heads,
    grad_heads,
    mixed_keys,
    mixed_query,
    turned_scores,
    attend_own,
    grads,
    attend,
    table,
    branch,
    keys_turned,
    wide,
    sem,
    in_sem,
):
    probs = (prob_a, prob_b, prob_c)

    def head_copies(h):
        pairs = [(s.at[h], p.at[h % 3]) for s, p in zip((prob_ra, prob_rb, prob_rc), probs)]
        lanes = pl.ds(h * 128, 128)
        for source, buf in ((keys_in, keys), (query_in, query), (heads_in, heads)):
            pairs.append((source.at[:, lanes], buf.at[:, lanes]))
        return [
            pltpu.make_async_copy(source, buf, sem.at[h % 2, n])
            for n, (source, buf) in enumerate(pairs)
        ]

    copies = [
        pltpu.make_async_copy(source, buf, in_sem.at[n])
        for n, (source, buf) in enumerate(
            ((table_ref, table), (branch_ref, branch), (attend_ref, attend))
        )
    ]
    for copy in copies[:2] + head_copies(0):
        copy.start()
    core, clips = layout_of(meta)
    part = meta[0]
    pieces = own_pieces(core, clips)
    turn = identity(256, 256)
    small_turn = identity(128, 128)
    ones = jnp.ones((8, 128), bf16)
    low_lanes = (lax.broadcasted_iota(jnp.int32, (1, HEAD_LANES), 1) & 127) < HD
    low_lane = low_lanes[:, 0:128]
    for copy in copies[:2]:
        copy.wait()
    for at in range(0, HALF, 256):
        rows = slice(at, at + 256)
        value = dot(branch[rows, :], table[1], NT)
        grad_heads[rows, :] = jnp.where(low_lanes, 0.0, value).astype(bf16)
    other_small = pl.ds(mult(1536 + (1 - core) * 256, 256), 256)
    mixed_keys[other_small, :] = jnp.zeros((256, HEAD_LANES), bf16)

    blocks = [
        (h, n, at)
        for h in range(HEADS)
        for n in range(3)
        for at in range(0, SEGMENTS[n][1], 256)
    ]
    inners = {}

    def head_stage(h):
        lanes = slice(h * 128, h * 128 + 128)
        for copy in head_copies(h):
            copy.wait()
        for copy in head_copies(h + 1) if h + 1 < HEADS else copies[2:]:
            copy.start()
        keys_turned[h % 2] = dot(small_turn, keys[:, lanes], NT).astype(bf16)
        out_wide = grad_heads[:, lanes].astype(f32)
        high, low = two_parts(out_wide * heads[:, lanes].astype(f32))
        inners[h] = (dot(ones, high, NT) + dot(ones, low, NT))[0:1]
        bias_rows[h] = jnp.sum(out_wide, axis=0, keepdims=True)

    def parts_of(block):
        h, n, at = block
        q_at, _, k_at, k_rows = SEGMENTS[n]
        lanes = slice(h * 128, h * 128 + 128)
        return slice(q_at + at, q_at + at + 256), slice(k_at, k_at + k_rows), lanes, k_rows

    def probs_stage(index):
        rows, k_range, lanes, k_rows = parts_of(blocks[index])
        if index == 0 or blocks[index - 1][0] != blocks[index][0]:
            head_stage(blocks[index][0])
        wide[index % 3, 0:k_rows] = dot(keys[k_range, lanes], grad_heads[rows, lanes], NT)

    def scores_stage(index):
        h, n, at = blocks[index]
        rows, _, _, k_rows = parts_of(blocks[index])
        for r in range(0, k_rows, 32):
            weights = probs[n][h % 3, r : r + 32, at : at + 256].astype(f32)
            value = (weights * (wide[index % 3, r : r + 32] - inners[h][:, rows])).astype(bf16)
            turned_scores[n, r : r + 32, at : at + 256] = value

    def query_stage(index):
        h, n, at = blocks[index]
        rows, k_range, lanes, k_rows = parts_of(blocks[index])
        value = dot(keys_turned[h % 2, :, k_range], turned_scores[n, 0:k_rows, at : at + 256], NN)
        value = dot(turn, (value * 0.125).astype(bf16), NT)
        value = jnp.where(low_lane, value, 0.0)
        mixed_query[rows, lanes] = value.astype(bf16)
        bias_rows[h] += jnp.sum(value, axis=0, keepdims=True)
        q_at, q_rows, k_at, _ = SEGMENTS[n]
        if at + 256 < q_rows:
            return
        rows = slice(q_at, q_at + q_rows)
        both = dot(query[rows, lanes], turned_scores[n, 0:k_rows, 0:q_rows], TT)
        both = both + dot(grad_heads[rows, lanes], probs[n][h % 3], TT)
        both = jnp.transpose(both)
        if n == 2:
            k_range = pl.ds(mult(1536 + core * 256, 256), 256)
        mixed_keys[k_range, lanes] = both.astype(bf16)

    probs_stage(0)
    for index in range(len(blocks)):
        if index + 1 < len(blocks):
            probs_stage(index + 1)
        if index:
            query_stage(index - 1)
        scores_stage(index)
    query_stage(len(blocks) - 1)

    copies[2].wait()
    for count, at, canon, _ in pieces:
        attend_own[at : at + count, :] = attend[pl.ds(mult(canon, 256), count), :]
    for i in range(4):
        rows = slice(CANON[i], CANON[i] + SIZES[i])
        grad_attend[rows, :] = dot(mixed_keys[rows, :], table[0], NN).astype(bf16)
    for count, at, canon, _ in pieces:
        rows = pl.ds(mult(canon, 256), count)
        value = dot(mixed_query[at : at + count, :], table[1], NN)
        grad_attend[rows, :] = (grad_attend[rows, :].astype(f32) + value).astype(bf16)
    sides = (
        dot(mixed_query[...], attend_own[...], TN) + dot(heads[...], branch[...], TN),
        dot(mixed_keys[...], attend[...], TN),
    )
    for g in range(GROUPS):
        at = jnp.bitwise_xor(part, g)
        for r in range(5):
            side, row = table_place(g * 5 + r)
            value = sides[1 - side][row : row + 64].astype(bf16)
            grads[lax.rem(at, 2), lax.div(at, 2), r * 64 : r * 64 + 64] = value
    send_ref[...] = grads[1]
    keep_ref[...] = grads[0]


def backward_block(meta, attend, probs, keys, query, heads, table, branch):
    return pl.pallas_call(
        backward_kernel,
        out_shape=(
            jax.ShapeDtypeStruct((SEQ, DP), bf16),
            jax.ShapeDtypeStruct((2, D, DP), bf16),
            jax.ShapeDtypeStruct((2, D, DP), bf16),
            jax.ShapeDtypeStruct((HEADS, 1, 128), f32),
        ),
        in_specs=[SMEM] + [ANY] * 9,
        out_specs=(VMEM,) * 4,
        scratch_shapes=[pltpu.VMEM((3,) + shape, bf16) for shape in PROBS]
        + [
            pltpu.VMEM((1792, HEAD_LANES), bf16),
            pltpu.VMEM((HALF, HEAD_LANES), bf16),
            pltpu.VMEM((HALF, HEAD_LANES), bf16),
            pltpu.VMEM((HALF, HEAD_LANES), bf16),
            pltpu.VMEM((SEQ, HEAD_LANES), bf16),
            pltpu.VMEM((HALF, HEAD_LANES), bf16),
            pltpu.VMEM((3, 1024, 512), bf16),
            pltpu.VMEM((HALF, DP), bf16),
            pltpu.VMEM((2, 2, D, DP), bf16),
            pltpu.VMEM((SEQ, DP), bf16),
            pltpu.VMEM((2, HEAD_LANES, DP), bf16),
            pltpu.VMEM((HALF, DP), bf16),
            pltpu.VMEM((2, 128, 1792), bf16),
            pltpu.VMEM((3, 1024, 256), f32),
            pltpu.SemaphoreType.DMA((2, 6)),
            pltpu.SemaphoreType.DMA((3,)),
        ],
        compiler_params=pltpu.CompilerParams(vmem_limit_bytes=58 * 2**20),
        cost_estimate=cost(16),
        name="backward_block",
    )(meta, attend, *probs, keys, query, heads, table, branch)


def owner_of(i, b):
    if i == 0:
        return b // 2, b % 2 * 256
    return (b, 512) if i == 1 else (i - 2, 768)


def norm_back_kernel(
    meta, own, other, second_own, second_oth, first, vec, rows_mlp, fc_rows, bias_rows, grad, rows_out
):
    core, clips = layout_of(meta)
    rows_out[...] = rows_mlp[...]
    for h in range(HEADS):
        rows_out[30:31, h * HD : h * HD + HD] = bias_rows[h][:, 0:HD]
        rows_out[31:32, h * HD : h * HD + HD] = bias_rows[h][:, HD:]
    for g in range(GROUPS):
        total = jnp.sum(fc_rows[:, g * D : g * D + D], axis=0, keepdims=True)
        rows_out[35 + g : 36 + g, 0:D] = total
    mask = lax.broadcasted_iota(jnp.int32, (1, DP), 1) < D
    for i in range(4):
        for b in range(SIZES[i] // 256):
            place = clips[i][0] + b * 256
            owner, at = owner_of(i, b)
            rows = slice(CANON[i] + b * 256, CANON[i] + b * 256 + 256)
            reach = (place >= core * HALF - 512) & (place < core * HALF + HALF + 512)

            @pl.when(reach)
            def _(place=place, owner=owner, at=at, rows=rows):
                grad_out = own[rows, :].astype(f32) + other[rows, :].astype(f32)
                normed, scale = norm_parts(first[rows, :], mask)
                second = jnp.where(
                    core == owner, second_own[at : at + 256, :], second_oth[at : at + 256, :]
                )
                whole = second.astype(f32) + norm_back(grad_out, normed, scale, vec[28:29, :])
                grad[rows, :] = whole

                @pl.when(lax.div(place, HALF) == core)
                def _():
                    rows_out[27:28, :] += jnp.sum(whole, axis=0, keepdims=True)
                    rows_out[28:29, :] += jnp.sum(grad_out * normed, axis=0, keepdims=True)
                    rows_out[29:30, :] += jnp.sum(grad_out, axis=0, keepdims=True)


def norm_backward(meta, own, other, second_own, second_oth, first, vec, rows):
    return pl.pallas_call(
        norm_back_kernel,
        out_shape=(
            jax.ShapeDtypeStruct((SEQ, DP), f32),
            jax.ShapeDtypeStruct((NVEC, DP), f32),
        ),
        in_specs=[SMEM] + [VMEM] * 9,
        out_specs=(VMEM,) * 2,
        compiler_params=pltpu.CompilerParams(vmem_limit_bytes=20 * 2**20),
        cost_estimate=cost(8),
        name="norm_backward",
    )(meta, own, other, second_own, second_oth, first, vec, *rows)


def conv_back_kernel(meta, grad, x_own, vec, rows_in, grad_rows, rows_out, padded, xw, vb):
    core, clips = layout_of(meta)
    clear_gaps(padded)
    tap_rows(vec, vb)
    turn = identity(256, 256)
    rows_out[...] = rows_in[...]
    for b in range(4):
        put_rows(xw, b * 32, dot(turn, x_own[:, b * 256 : b * 256 + 256], NT))
    for i in range(4):
        for b in range(SIZES[i] // 256):
            at = CANON[i] + b * 256
            put_rows(padded, PTILES[i] + b * 32, grad[at : at + 256, :])
    blocks = [block_of(clips, core * HALF + b * 256) for b in range(4)]
    for c in range(3):
        sums = tuple(jnp.zeros((8, 128), f32) for _ in range(27))
        for b, (width, plane, local, tile) in enumerate(blocks):
            not_last, not_first = columns(2, width)

            def step(n, sums, b=b, c=c, block=blocks[b], not_last=not_last, not_first=not_first):
                width, plane, local, tile = block
                sums = list(sums)
                x = xw[c, pl.ds(b * 32 + n * 2, 2)]
                shifted = (to_right(x, not_last), x, to_left(x, not_first))
                parts = [None] * 3
                at = tile + n * 2
                for k, value in neighbours(padded, c, at, 2, width, plane, local + n * 2):
                    for dc in range(3):
                        mirror = 26 - (k + dc)
                        term = value * vb[mirror, c]
                        parts[dc] = term if parts[dc] is None else parts[dc] + term
                        product = value * shifted[dc]
                        sums[mirror] = sums[mirror] + (product[0] + product[1])
                total = padded[c, pl.ds(at, 2)] + parts[1]
                total = total + to_left(parts[0], not_first)
                total = total + to_right(parts[2], not_last)
                rows = pl.ds(mult(b * 256 + n * 16, 16), 16)
                grad_rows[rows, c * 128 : c * 128 + 128] = total.reshape(16, 128).astype(bf16)
                return tuple(sums)

            sums = lax.fori_loop(0, 16, step, sums)
        for k in range(27):
            lanes = slice(c * 128, c * 128 + 128)
            rows_out[k : k + 1, lanes] = jnp.sum(sums[k], axis=0, keepdims=True)


def conv_backward(meta, grad, x_own, vec, rows):
    return pl.pallas_call(
        conv_back_kernel,
        out_shape=(
            jax.ShapeDtypeStruct((HALF, DP), bf16),
            jax.ShapeDtypeStruct((NVEC, DP), f32),
        ),
        in_specs=[SMEM] + [VMEM] * 4,
        out_specs=(VMEM,) * 2,
        scratch_shapes=[
            pltpu.VMEM((3, ALL_TILES, 8, 128), f32),
            pltpu.VMEM((3, HALF // 8, 8, 128), f32),
            pltpu.VMEM((27, 3, 8, 128), f32),
        ],
        compiler_params=pltpu.CompilerParams(vmem_limit_bytes=20 * 2**20),
        cost_estimate=cost(11),
        name="conv_backward",
    )(meta, grad, x_own, vec, rows)


def turn_kernel(meta, out_own, out_oth, grad_rows, block_out, input_grad):
    core, clips = layout_of(meta)
    turn = identity(D, DP)
    mask = lax.broadcasted_iota(jnp.int32, (1, DP), 1) < D
    for i in range(4):
        for b in range(SIZES[i] // 256):
            place = clips[i][0] + b * 256
            owner, at = owner_of(i, b)
            mine = lax.div(place, HALF) == core
            lanes = pl.ds(mult(lax.rem(place, HALF), 256), 256)
            for source, here in ((out_own, core == owner), (out_oth, core != owner)):

                @pl.when(mine & here)
                def _(source=source, at=at, lanes=lanes):
                    value = jnp.where(mask, source[at : at + 256, :].astype(f32), 0.0)
                    block_out[:, lanes] = dot(turn, value.astype(bf16), NT).astype(bf16)

    for b in range(4):
        rows = slice(b * 256, b * 256 + 256)
        value = jnp.where(mask, grad_rows[rows, :].astype(f32), 0.0).astype(bf16)
        input_grad[:, rows] = dot(turn, value, NT).astype(bf16)


def turned_outputs(meta, out_own, out_oth, grad_rows):
    shape = jax.ShapeDtypeStruct((D, HALF), bf16)
    return pl.pallas_call(
        turn_kernel,
        out_shape=(shape, shape),
        in_specs=[SMEM] + [VMEM] * 3,
        out_specs=(VMEM,) * 2,
        compiler_params=pltpu.CompilerParams(vmem_limit_bytes=12 * 2**20),
        cost_estimate=cost(3),
        name="turned_outputs",
    )(meta, out_own, out_oth, grad_rows)


def spread_kernel(meta, fc_keep, fc_recv, table_keep, table_recv, *refs):
    slots = refs[-1]
    outs = refs[:-1]
    _, ranks, owned = slots.shape[:3]
    slots[...] = jnp.zeros_like(slots)
    for far in range(2):
        for first_tile, count, keep, recv in (
            (0, D // TR, table_keep, table_recv),
            (D // TR, 2 * D // TR, fc_keep, fc_recv),
        ):

            for j in range(count):
                rows = slice(j * TR, j * TR + TR)
                value = keep[far, rows, :].astype(f32) + recv[far, rows, :].astype(f32)
                slot = meta[META_TILES + first_tile + j]
                slots[far, lax.div(slot, owned), lax.rem(slot, owned)] = value[:, 0:D]
    cut = owned - owned // 2
    outs[0][...] = slots[0, :, 0:cut]
    outs[1][...] = slots[1, :, 0:cut].astype(bf16)
    if cut < owned:
        outs[2][...] = slots[:, 0 : ranks // 2, cut:]
        outs[3][...] = slots[:, ranks // 2 :, cut:].astype(bf16)


def spread(meta, ranks, *grads):
    owned = SLOTS // ranks
    cut = owned - owned // 2
    shapes = [(ranks, cut, TR, D)]
    if cut < owned:
        shapes.append((2, ranks // 2, owned - cut, TR, D))
    out_shape = [jax.ShapeDtypeStruct(shape, kind) for shape in shapes for kind in (f32, bf16)]
    return pl.pallas_call(
        spread_kernel,
        out_shape=out_shape,
        in_specs=[SMEM] + [VMEM] * 4,
        out_specs=[VMEM] * len(out_shape),
        scratch_shapes=[pltpu.VMEM((2, ranks, owned, TR, D), f32)],
        compiler_params=pltpu.CompilerParams(vmem_limit_bytes=24 * 2**20),
        cost_estimate=cost(3),
        name="spread_tiles",
    )(meta, *grads)


def halves_kernel(count, *refs):
    for n in range(count):
        keep, recv = refs[2 * n], refs[2 * n + 1]
        out_keep, out_send = refs[2 * count + 2 * n], refs[2 * count + 2 * n + 1]
        half = keep.shape[0] // 2
        out_keep[...] = keep[0:half] + recv[0:half].astype(f32)
        out_send[...] = (keep[half:] + recv[half:].astype(f32)).astype(bf16)


def halves(pairs):
    flat = [value for pair in pairs for value in pair]
    out_shape = []
    for keep, _ in pairs:
        shape = (keep.shape[0] // 2,) + keep.shape[1:]
        out_shape += [jax.ShapeDtypeStruct(shape, f32), jax.ShapeDtypeStruct(shape, bf16)]
    return pl.pallas_call(
        functools.partial(halves_kernel, len(pairs)),
        out_shape=out_shape,
        in_specs=[VMEM] * len(flat),
        out_specs=[VMEM] * len(out_shape),
        compiler_params=pltpu.CompilerParams(vmem_limit_bytes=16 * 2**20),
        cost_estimate=cost(1.5),
        name="halves",
    )(*flat)


def split_kernel(counts, *refs):
    terms = refs[: sum(counts)]
    outs = refs[sum(counts) :]
    size = outs[0].shape[0]
    for q, out in enumerate(outs):
        at, low = 0, 0
        for count in counts:
            rows = slice(q * size, q * size + size)
            value = terms[at][rows]
            for other in terms[at + 1 : at + count]:
                value = value + other[rows].astype(f32)
            width = value.shape[1]
            out[:, low : low + width] = value.astype(out.dtype)
            at, low = at + count, low + width


def split(groups, pieces):
    flat = [value for group in groups for value in group]
    owned = sum(group[0].shape[1] for group in groups)
    shape = (flat[0].shape[0] // pieces, owned, TR, D)
    out_shape = [jax.ShapeDtypeStruct(shape, f32)]
    out_shape += [jax.ShapeDtypeStruct(shape, bf16)] * (pieces - 1)
    return pl.pallas_call(
        functools.partial(split_kernel, tuple(len(group) for group in groups)),
        out_shape=out_shape,
        in_specs=[VMEM] * len(flat),
        out_specs=[VMEM] * pieces,
        compiler_params=pltpu.CompilerParams(vmem_limit_bytes=16 * 2**20),
        cost_estimate=cost(1.5),
        name="split_slots",
    )(*flat)


def dot_parts(a, b, dims):
    return dot(a[0], b[0], dims) + (dot(a[1], b[0], dims) + dot(a[0], b[1], dims))


def dot_low(a, b, dims):
    rows = a.shape[0]
    both = dot(jnp.concatenate(two_parts(a), axis=0), b, dims)
    return both[:rows] + both[rows:]


def bases_kernel(left, right, left_out, right_out):
    owned = left.shape[0]
    rows = owned * TR
    at = [lax.broadcasted_iota(jnp.int32, (TR, rows), n) for n in range(2)]
    repeat = jnp.where(at[0] == (at[1] & (TR - 1)), 1.0, 0.0).astype(bf16)
    at = [lax.broadcasted_iota(jnp.int32, (rows, rows), n) // TR for n in range(2)]
    for n, piece in enumerate(two_parts(left[...].reshape(rows, TR))):
        left_out[n] = jnp.where(at[0] == at[1], dot(piece, repeat, NN), 0.0).astype(bf16)
    right_out[...] = right[...].astype(bf16)


def split_bases(left, right):
    owned = left.shape[0]
    return pl.pallas_call(
        bases_kernel,
        out_shape=(
            jax.ShapeDtypeStruct((2, owned * TR, owned * TR), bf16),
            jax.ShapeDtypeStruct(right.shape, bf16),
        ),
        in_specs=[VMEM] * 2,
        out_specs=(VMEM,) * 2,
        compiler_params=pltpu.CompilerParams(vmem_limit_bytes=24 * 2**20),
        cost_estimate=cost(3),
        name="split_bases",
    )(left, right)


def soap_kernel(count, corr, *refs):
    grads = refs[:count]
    masters, left, right, first, second, out_w, out_m, out_v, wide = refs[count:]
    grad = grads[0][0]
    for other in grads[1:]:
        grad = grad + other[0].astype(f32)
    owned = grad.shape[0]
    rows = owned * TR
    sides = (left[0], left[1])
    turned = dot_parts(sides, two_parts(grad.reshape(rows, D)), TN)
    for s in range(owned):
        rotated = dot_low(turned[s * TR : s * TR + TR], right[s], NN)
        new_first = beta_one * first[s] + (1.0 - beta_one) * rotated
        new_second = beta_two * second[s] + (1.0 - beta_two) * rotated * rotated
        out_m[s] = new_first
        out_v[s] = new_second
        direction = new_first / corr[0] / (jnp.sqrt(new_second / corr[1]) + adam_eps)
        wide[s * TR : s * TR + TR] = dot_low(direction, right[s], NT)
    back = dot_parts(sides, two_parts(wide[...]), NN).reshape(owned, TR, D)
    out_w[...] = masters[...] - matrix_rate * (back + matrix_decay * masters[...])


def soap(corr, grads, masters, bases, first, second):
    shape = jax.ShapeDtypeStruct(masters.shape, f32)
    return pl.pallas_call(
        functools.partial(soap_kernel, len(grads)),
        out_shape=(shape, shape, shape),
        in_specs=[SMEM] + [VMEM] * (len(grads) + 5),
        out_specs=(VMEM,) * 3,
        scratch_shapes=[pltpu.VMEM((masters.shape[0] * TR, D), f32)],
        compiler_params=pltpu.CompilerParams(vmem_limit_bytes=24 * 2**20),
        cost_estimate=cost(5),
        name="tile_update",
    )(corr, *grads, masters, *bases, first, second)


def flipped(value, axes, bit):
    size = lax.axis_size(axes)
    return lax.ppermute(value, axes, [(i, i ^ bit) for i in range(size)])


def tied(*values):
    return lax.optimization_barrier(values)


def masks_of(bits):
    return [0, bits[0]] if len(bits) == 1 else [0, bits[1], bits[0], bits[0] | bits[1]]


def on_device(
    block_input,
    cotangent,
    clip_starts,
    clip_shapes,
    tile_slot,
    masters,
    left_bases,
    right_bases,
    first_moment,
    second_moment,
    vectors,
    vector_first,
    vector_second,
    step_count,
):
    part = lax.axis_index("tp")
    rank = lax.axis_index("dp")
    ranks, groups = lax.axis_size("dp"), lax.axis_size("tp")
    bits = [1 << n for n in range(ranks.bit_length() - 1)]
    near, far = bits[0], [tuple(bits[n : n + 2]) for n in range(1, len(bits), 2)]
    owned = masters.shape[1]
    cut = owned - owned // 2

    relative = jnp.bitwise_xor(tile_slot // owned, rank)
    position = sum(
        ((relative >> n) & 1) << (len(bits) - 1 - n) for n in range(len(bits))
    ) * owned + tile_slot % owned
    meta = jnp.concatenate(
        [part[None].astype(jnp.int32), clip_starts.reshape(-1), clip_shapes.reshape(-1), position]
    )
    vec = jnp.pad(vectors, ((0, 0), (0, DP - D)))
    vec = vec.at[29, D].set(1.0).at[34, D].set(1.0)
    bias_qv = jnp.concatenate(
        [vectors[30].reshape(HEADS, HD), vectors[31].reshape(HEADS, HD)], axis=1
    ).reshape(1, HEAD_LANES)
    bias_one = vectors[35:39].reshape(1, FF)

    x_own = block_input.T
    cot_own = cotangent.T
    x_oth = flipped(x_own, "tp", 1)
    cot_oth = flipped(cot_own, "tp", 1)
    held = masters[0].astype(bf16)[None]
    for group in reversed(far):
        held = jnp.concatenate([flipped(held, "dp", m) if m else held for m in masks_of(group)])
    held, meta, vec, bias_qv, bias_one, x_oth = tied(held, meta, vec, bias_qv, bias_one, x_oth)
    near_first = held[:, :cut]
    near_first = jnp.stack([near_first, flipped(near_first, "dp", near)])
    early = [(0, ((0, 0), (0, 1)), near_first)]
    late = [(0, ((2, 0), (2, 1)), flipped(near_first, "tp", 2))]
    if cut < owned:
        far_first = held[:, cut:]
        far_first = jnp.stack([far_first, flipped(far_first, "tp", 2)])
        early.append((cut, ((0, 0), (2, 0)), far_first))
        late.append((cut, ((0, 1), (2, 1)), flipped(far_first, "dp", near)))
    attend, first = conv_forward(meta, x_own, x_oth, vec, early[-1][2])
    attend, *values = tied(attend, *[value for _, _, value in late])
    pieces = early + [(low, entries, value) for (low, entries, _), value in zip(late, values)]
    for low, entries, value in list(pieces):
        entries = tuple((q + 1, side) for q, side in entries)
        pieces.append((low, entries, flipped(value, "tp", 1)))

    (
        prob_a,
        prob_b,
        prob_c,
        keys,
        query,
        heads,
        table,
        block_out,
        branch,
        fc_send,
        fc_keep,
        rows_mlp,
        fc_rows,
    ) = forward_block(
        meta,
        attend,
        first,
        vec,
        bias_qv,
        bias_one,
        cot_own,
        cot_oth,
        [value for _, _, value in pieces],
        tuple((low, entries) for low, entries, _ in pieces),
        ranks,
    )
    block_oth = flipped(block_out, "tp", 1)
    branch_oth = flipped(branch, "tp", 1)
    fc_recv = flipped(fc_send, "tp", 1)
    grad_attend, table_send, table_keep, bias_rows = backward_block(
        meta, attend, (prob_a, prob_b, prob_c), keys, query, heads, table, branch
    )
    grad_attend, table_send, block_oth, branch_oth, fc_recv, left, right = tied(
        grad_attend, table_send, block_oth, branch_oth, fc_recv, left_bases[0], right_bases[0]
    )
    grad_attend_oth = flipped(grad_attend, "tp", 1)
    table_recv = flipped(table_send, "tp", 1)
    bases = split_bases(left, right)
    table_recv, *bases = tied(table_recv, *bases)

    spreads = spread(meta, ranks, fc_keep, fc_recv, table_keep, table_recv)
    pairs = [(spreads[0], flipped(spreads[1], "tp", 2))]
    if cut < owned:
        pairs.append((spreads[2], flipped(spreads[3], "dp", near)))
    grad_first, vector_rows = norm_backward(
        meta,
        grad_attend,
        grad_attend_oth,
        branch,
        branch_oth,
        first,
        vec,
        (rows_mlp, fc_rows, bias_rows),
    )
    grad_first, *recvs = tied(grad_first, *[recv for _, recv in pairs])
    result = halves([(keep, recv) for (keep, _), recv in zip(pairs, recvs)])
    grad_first, *result = tied(grad_first, *result)
    terms = [(result[0], flipped(result[1], "dp", near))]
    if cut < owned:
        terms.append((result[2][0], flipped(result[3], "tp", 2)[0]))
    grad_rows, vector_grad = conv_backward(meta, grad_first, x_own, vec, vector_rows)
    vector_grad, *recvs = tied(vector_grad, *[recv for _, recv in terms])
    terms = [(keep, recv) for (keep, _), recv in zip(terms, recvs)]
    for group in far:
        masks = masks_of(group)
        pieces = split(terms, len(masks))
        terms = [tuple(flipped(v, "dp", m) if m else v for v, m in zip(pieces, masks))]

    vector_grad, grad_rows = tied(vector_grad + flipped(vector_grad, "tp", 1), grad_rows)
    block_output, input_grad = turned_outputs(meta, block_out, block_oth, grad_rows)
    for axes, flips in [(("dp", "tp"), (2, near * groups))] + [("dp", group) for group in far]:
        values = [flipped(vector_grad, axes, m) if m else vector_grad for m in masks_of(flips)]
        while len(values) > 1:
            values = [values[n] + values[n + 1] for n in range(0, len(values), 2)]
        vector_grad = values[0]
    vector_grad = vector_grad[:, :D]

    steps = step_count[0].astype(f32)
    corr_one = 1.0 - jnp.power(beta_one, steps)
    corr_two = 1.0 - jnp.power(beta_two, steps)
    new_masters, new_first, new_second = soap(
        jnp.stack([corr_one, corr_two]),
        terms[0],
        masters[0],
        bases,
        first_moment[0],
        second_moment[0],
    )
    new_vector_first = beta_one * vector_first + (1.0 - beta_one) * vector_grad
    new_vector_second = beta_two * vector_second + (1.0 - beta_two) * vector_grad * vector_grad
    direction = new_vector_first / corr_one
    direction = direction / (jnp.sqrt(new_vector_second / corr_two) + adam_eps)
    return (
        block_output.T,
        input_grad.T,
        new_masters[None],
        new_first[None],
        new_second[None],
        vectors - vector_rate * direction,
        new_vector_first,
        new_vector_second,
    )


def solution(mesh):
    tokens = P(("dp", "tp"), None)
    tiles = P("tp", "dp", None, None)
    in_specs = (
        tokens,
        tokens,
        P("dp", None),
        P("dp", None, None),
        P(),
        tiles,
        tiles,
        tiles,
        tiles,
        tiles,
        P(),
        P(),
        P(),
        P(),
    )
    out_specs = (tokens, tokens, tiles, tiles, tiles, P(), P(), P())
    return jax.shard_map(
        on_device, mesh=mesh, in_specs=in_specs, out_specs=out_specs, check_vma=False
    )
```

```python
import functools

import jax
import jax.numpy as jnp
from jax import lax
from jax.experimental import pallas as pl
from jax.experimental.pallas import tpu as pltpu
from jax.sharding import PartitionSpec as P

D = 320
DP = 384
HEADS = 5
HD = 64
FF = 1280
SEQ = 2048
HALF = SEQ // 2
TR = 16
SLOTS = 64
TILES = 60
NVEC = 40
GROUPS = FF // D

norm_eps = 1e-06
beta_one = 0.9
beta_two = 0.99
adam_eps = 1e-08
matrix_rate = 0.1
matrix_decay = 0.05
vector_rate = 0.5

SIZES = (1024, 512, 256, 256)
CANON = (0, 1024, 1536, 1792)
GAP = 34
PTILES = (GAP, 2 * GAP + 128, 3 * GAP + 192, 4 * GAP + 224)
ALL_TILES = 5 * GAP + 256
WIDTHS = (128, 128, 64)

f32 = jnp.float32
bf16 = jnp.bfloat16
NN = (((1,), (0,)), ((), ()))
NT = (((1,), (1,)), ((), ()))
TN = (((0,), (0,)), ((), ()))
TT = (((0,), (1,)), ((), ()))

SMEM = pl.BlockSpec(memory_space=pltpu.SMEM)
VMEM = pl.BlockSpec(memory_space=pltpu.VMEM)
ANY = pl.BlockSpec(memory_space=pltpu.HBM)
LOOSE = pl.BlockSpec(memory_space=pl.ANY)


def dot(a, b, dims):
    return lax.dot_general(a, b, dims, preferred_element_type=f32)


def cost(microseconds):
    return pl.CostEstimate(flops=0, bytes_accessed=int(microseconds * 3.5e6), transcendentals=0)


def mult(value, step):
    return pl.multiple_of(value, step)


META_STARTS = 1
META_SHAPES = 9
META_TILES = 33


def layout_of(meta):
    part = meta[0]
    core = lax.rem(part, 2)
    row = lax.div(part, 2)
    starts = [meta[META_STARTS + row * 4 + i] for i in range(4)]
    shapes = [[meta[META_SHAPES + row * 12 + 3 * i + k] for k in range(3)] for i in range(4)]
    counts = [s[0] * s[1] * s[2] for s in shapes]
    seen = jnp.int32(0)
    marks = [[], [], [], []]
    for i in range(4):
        small = (counts[i] == 256).astype(jnp.int32)
        marks[0].append((counts[i] == 1024).astype(jnp.int32))
        marks[1].append((counts[i] == 512).astype(jnp.int32))
        marks[2].append(small * (1 - seen))
        marks[3].append(small * seen)
        seen = jnp.maximum(seen, small)
    clips = []
    for mark in marks:
        pick = lambda values: sum(m * v for m, v in zip(mark, values))
        clips.append((pick(starts), pick([s[1] for s in shapes]), pick([s[2] for s in shapes])))
    return core, clips


def own_pieces(core, clips):
    small_start = jnp.where(core == 0, clips[2][0], clips[3][0])
    return (
        (512, 0, core * 512, clips[0][0] + core * 512),
        (256, 512, 1024 + core * 256, clips[1][0] + core * 256),
        (256, 768, 1536 + core * 256, small_start),
    )


def identity(rows, columns):
    at = [lax.broadcasted_iota(jnp.int32, (rows, columns), n) for n in range(2)]
    return jnp.where(at[0] == at[1], 1.0, 0.0).astype(bf16)


def clear_gaps(padded):
    for at in (0,) + tuple(p + s // 8 for p, s in zip(PTILES, SIZES)):
        padded[:, at : at + GAP] = jnp.zeros((3, GAP, 8, 128), f32)


def put_rows(padded, tile, value):
    for c, width in enumerate(WIDTHS):
        piece = value[:, c * 128 : c * 128 + width].reshape(32, 8, width)
        padded[c, pl.ds(tile, 32), :, 0:width] = piece


def tap_rows(vec, vb):
    for k in range(27):
        for c in range(3):
            vb[k, c] = jnp.broadcast_to(vec[k : k + 1, c * 128 : c * 128 + 128], (8, 128))


def block_of(clips, place):
    index = jnp.int32(0)
    for i in range(4):
        begin = clips[i][0]
        index = jnp.where((place >= begin) & (place < begin + SIZES[i]), i, index)

    def pick(values):
        high = jnp.where(index == 2, values[2], values[3])
        return jnp.where(index == 0, values[0], jnp.where(index == 1, values[1], high))

    width = lax.div(pick([c[2] for c in clips]), 8)
    plane = pick([c[1] for c in clips]) * width
    local = lax.div(place - pick([c[0] for c in clips]), 8)
    return width, plane, local, local + pick([jnp.int32(p) for p in PTILES])


def neighbours(padded, c, tile, tiles, width, plane, local):
    place = (lax.broadcasted_iota(jnp.int32, (tiles, 8, 128), 0) + local) & (plane - 1)
    inside = (place >= width, None, place < plane - width)
    for df in range(3):
        for dr in range(3):
            value = padded[c, pl.ds(tile + (df - 1) * plane + (dr - 1) * width, tiles)]
            yield 9 * df + 3 * dr, value if dr == 1 else jnp.where(inside[dr], value, 0.0)


def columns(tiles, width):
    at = lax.broadcasted_iota(jnp.int32, (tiles * 8, 128), 0) & (width * 8 - 1)
    return at != width * 8 - 1, at != 0


def to_left(value, not_first):
    tiles = value.shape[0]
    rolled = pltpu.roll(value.reshape(tiles * 8, 128), 1, 0)
    return jnp.where(not_first, rolled, 0.0).reshape(tiles, 8, 128)


def to_right(value, not_last):
    tiles = value.shape[0]
    rolled = pltpu.roll(value.reshape(tiles * 8, 128), tiles * 8 - 1, 0)
    return jnp.where(not_last, rolled, 0.0).reshape(tiles, 8, 128)


UNIT = 8


def conv_kernel(
    meta, x_own, x_oth, vec, after, attend_out, first_out, padded, vb, first, attend, sem
):
    core, clips = layout_of(meta)
    clear_gaps(padded)
    tap_rows(vec, vb)
    turn = identity(256, 256)
    for half, ref in ((core, x_own), (1 - core, x_oth)):
        for b in range(4):
            tile = block_of(clips, half * HALF + b * 256)[3]
            put_rows(padded, tile, dot(turn, ref[:, b * 256 : b * 256 + 256], NT))
    copies = []
    mask = lax.broadcasted_iota(jnp.int32, (1, DP), 1) < D
    for i in range(4):
        width = lax.div(clips[i][2], 8)
        plane = clips[i][1] * width

        def unit(u, carry, i=i, width=width, plane=plane):
            tile = u * UNIT + PTILES[i]
            not_last, not_first = columns(UNIT, width)
            rows = pl.ds(mult(u * (8 * UNIT) + CANON[i], 8 * UNIT), 8 * UNIT)
            for c in range(3):
                sums = [None] * 3
                for k, value in neighbours(padded, c, tile, UNIT, width, plane, u * UNIT):
                    for dc in range(3):
                        term = value * vb[k + dc, c]
                        sums[dc] = term if sums[dc] is None else sums[dc] + term
                total = padded[c, pl.ds(tile, UNIT)] + vec[27:28, c * 128 : c * 128 + 128]
                total = total + sums[1]
                total = total + to_left(sums[0], not_first)
                total = total + to_right(sums[2], not_last)
                first[rows, c * 128 : c * 128 + 128] = total.reshape(8 * UNIT, 128)
            return carry

        lax.fori_loop(0, SIZES[i] // (8 * UNIT), unit, 0)
        rows = pl.ds(CANON[i], SIZES[i])
        copies.append(pltpu.make_async_copy(first.at[rows], first_out.at[rows], sem.at[0, i]))
        copies[-1].start()

        def norm(n, carry, i=i):
            rows = pl.ds(mult(CANON[i] + n * 256, 256), 256)
            normed, _ = norm_parts(first[rows, :], mask)
            attend[rows, :] = (normed * vec[28:29, :] + vec[29:30, :]).astype(bf16)
            return carry

        lax.fori_loop(0, SIZES[i] // 256, norm, 0)
        copies.append(pltpu.make_async_copy(attend.at[rows], attend_out.at[rows], sem.at[1, i]))
        copies[-1].start()
    for copy in copies:
        copy.wait()


def conv_forward(meta, x_own, x_oth, vec, after):
    return pl.pallas_call(
        conv_kernel,
        out_shape=(
            jax.ShapeDtypeStruct((SEQ, DP), bf16),
            jax.ShapeDtypeStruct((SEQ, DP), f32),
        ),
        in_specs=[SMEM, VMEM, VMEM, VMEM, LOOSE],
        out_specs=(ANY, ANY),
        scratch_shapes=[
            pltpu.VMEM((3, ALL_TILES, 8, 128), f32),
            pltpu.VMEM((27, 3, 8, 128), f32),
            pltpu.VMEM((SEQ, DP), f32),
            pltpu.VMEM((SEQ, DP), bf16),
            pltpu.SemaphoreType.DMA((2, 4)),
        ],
        compiler_params=pltpu.CompilerParams(vmem_limit_bytes=54 * 2**20),
        cost_estimate=cost(12),
        name="conv_forward",
    )(meta, x_own, x_oth, vec, after)


def two_parts(value):
    high = value.astype(bf16)
    return high, (value - high.astype(f32)).astype(bf16)


def norm_parts(values, mask):
    values = jnp.where(mask, values, 0.0)
    mean = jnp.sum(values, axis=-1, keepdims=True) * (1.0 / D)
    center = jnp.where(mask, values - mean, 0.0)
    scale = lax.rsqrt(jnp.sum(center * center, axis=-1, keepdims=True) * (1.0 / D) + norm_eps)
    return center * scale, scale


def norm_back(grad, normed, scale, gain):
    scaled = grad * gain
    mean = jnp.sum(scaled, axis=-1, keepdims=True) * (1.0 / D)
    inner = jnp.sum(scaled * normed, axis=-1, keepdims=True) * (1.0 / D)
    return scale * (scaled - mean - normed * inner)


def phi_parts(v):
    density = jnp.exp2(v * v * -0.7213475204444817) * 0.3989422804014327
    return 0.5 + 0.5 * lax.erf(v * 0.7071067811865476), density


SEGMENTS = ((0, 512, 0, 1024), (512, 256, 1024, 512), (768, 256, 1536, 256))
PROBS = ((1024, 512), (512, 256), (256, 256))
HEAD_LANES = HEADS * 128
VECTOR_TILES = -(-NVEC // TR)


def table_place(run):
    head, kind = divmod(run, 4)
    return (1, 0, 0, 1)[kind], head * 128 + (0, 0, 64, 64)[kind]


def forward_kernel(places_of, *refs):
    meta, attend_ref, first, vec, bias_qv, bias_one, cot_own, cot_oth = refs[:8]
    held = refs[8 : 8 + len(places_of)]
    refs = refs[8 + len(places_of) :]
    prob_refs, keys_ref, query_ref, heads_ref = refs[:3], refs[3], refs[4], refs[5]
    table_ref, block_ref, branch_ref, send_ref, keep_ref, rows_out, fc_rows = refs[6:13]
    (
        prob_a,
        prob_b,
        prob_c,
        keys,
        query,
        heads,
        table,
        block_out,
        branch,
        grads,
        wide,
        pres,
        backs,
        second,
        tiles,
        fc_one,
        fc_two,
        hidden,
        grad_pre,
        mlp_in,
        cot_low,
        attend,
        keys_turned,
        sem,
        prob_sem,
        out_sem,
    ) = refs[13:]
    core, clips = layout_of(meta)
    part = meta[0]
    pieces = own_pieces(core, clips)
    copies = []
    for ref, (low, entries) in zip(held, places_of):
        count, owned = ref.shape[1:3]
        for n, (group, side) in enumerate(entries):
            into = tiles.at[group, pl.ds(side * count, count), pl.ds(low, owned)]
            copies.append(pltpu.make_async_copy(ref.at[n], into, sem.at[len(copies)]))
    held_count = len(copies)
    copies.append(pltpu.make_async_copy(attend_ref, attend, sem.at[len(copies)]))
    for count, at, canon, _ in pieces:
        copies.append(
            pltpu.make_async_copy(
                first.at[pl.ds(mult(canon, 256), count)],
                second.at[pl.ds(at, count)],
                sem.at[len(copies)],
            )
        )
    for copy in copies[: held_count + 1]:
        copy.start()
    outs = []

    def send_out(source, target):
        outs.append(pltpu.make_async_copy(source, target, out_sem.at[len(outs)]))
        outs[-1].start()

    turn = identity(256, 256)
    cot_low[:, 256:DP] = jnp.zeros((HALF, 128), bf16)
    for n in range(4):
        place = (pieces[0][3], pieces[0][3] + 256, pieces[1][3], pieces[2][3])[n]
        lanes = pl.ds(mult(lax.rem(place, HALF), 256), 256)
        mine = lax.div(place, HALF) == core
        for ref, here in ((cot_own, mine), (cot_oth, jnp.logical_not(mine))):

            @pl.when(here)
            def _(ref=ref, n=n, lanes=lanes):
                value = dot(turn, ref[:, lanes], NT).astype(bf16)
                cot_low[n * 256 : n * 256 + 256, 0:D] = value

    table[:, :, 256:DP] = jnp.zeros((2, HEAD_LANES, 128), bf16)
    for ref in (fc_one, fc_two):
        ref[:, 256:DP] = jnp.zeros((FF, 128), bf16)
    rows_out[...] = jnp.zeros_like(rows_out)
    fc_rows[...] = jnp.zeros_like(fc_rows)
    for copy in copies[:held_count]:
        copy.wait()
    for copy in copies[held_count + 1 :]:
        copy.start()
    owned = tiles.shape[2]

    def tile_of(group, tile):
        slot = meta[META_TILES + tile]
        at = jnp.bitwise_xor(part, group)
        return tiles[at, lax.div(slot, owned), lax.rem(slot, owned)]

    for g in range(GROUPS):
        for j in range(D // TR):
            side, row = table_place(g * 5 + j // 4)
            row = row + j % 4 * TR
            table[side, row : row + TR, 0:D] = tile_of(g, j)
    send_out(table, table_ref)

    mask = lax.broadcasted_iota(jnp.int32, (1, DP), 1) < D
    low_lanes = (lax.broadcasted_iota(jnp.int32, (1, HEAD_LANES), 1) & 127) < HD
    low_lane = low_lanes[:, 0:128]
    bias_q = jnp.where(low_lanes, bias_qv[...], 0.0)
    bias_v = bias_qv[...] - bias_q
    small_rows = pl.ds(mult(1536 + core * 256, 256), 256)
    copies[held_count].wait()
    for at in range(0, 1536, 512):
        value = dot(attend[at : at + 512, :], table[0], NT) + bias_v
        keys[at : at + 512, :] = value.astype(bf16)
    keys[1536:1792, :] = (dot(attend[small_rows, :], table[0], NT) + bias_v).astype(bf16)
    for count, at, canon, _ in pieces:
        value = dot(attend[pl.ds(mult(canon, 256), count), :], table[1], NT) + bias_q
        query[at : at + count, :] = jnp.where(low_lanes, value, 0.0).astype(bf16) * bf16(0.125)
    send_out(keys, keys_ref)
    send_out(query, query_ref)
    small_turn = identity(128, 128)
    for h in range(HEADS):
        lanes = slice(h * 128, h * 128 + 128)
        keys_turned[lanes, :] = dot(small_turn, keys[:, lanes], NT).astype(bf16)

    probs = (prob_a, prob_b, prob_c)

    def prob_copies(h):
        return [
            pltpu.make_async_copy(buf.at[h % 2], out.at[h], prob_sem.at[h % 2, n])
            for n, (buf, out) in enumerate(zip(probs, prob_refs))
        ]

    blocks = [
        (h, n, at)
        for h in range(HEADS)
        for n in range(3)
        for at in range(0, SEGMENTS[n][1], 256)
    ]

    def parts_of(block):
        h, n, at = block
        q_at, _, k_at, k_rows = SEGMENTS[n]
        lanes = slice(h * 128, h * 128 + 128)
        return slice(q_at + at, q_at + at + 256), slice(k_at, k_at + k_rows), lanes, k_rows

    def score_stage(index):
        rows, k_range, lanes, k_rows = parts_of(blocks[index])
        wide[index % 3, 0:k_rows] = dot(keys[k_range, lanes], query[rows, lanes], NT)

    def softmax_stage(index):
        h, n, at = blocks[index]
        k_rows = SEGMENTS[n][3]
        if h >= 2 and n == 0 and at == 0:
            for copy in prob_copies(h - 2):
                copy.wait()
        scores = wide.at[index % 3]
        peak = jnp.max(scores[0:k_rows], axis=0, keepdims=True)
        total = jnp.zeros((8, 256), f32)
        for r in range(0, k_rows, 32):
            weights = jnp.exp(scores[r : r + 32] - peak)
            scores[r : r + 32] = weights
            total = total + jnp.sum(weights.reshape(4, 8, 256), axis=0)
        inverse = 1.0 / jnp.sum(total, axis=0, keepdims=True)
        for r in range(0, k_rows, 32):
            value = (scores[r : r + 32] * inverse).astype(bf16)
            probs[n][h % 2, r : r + 32, at : at + 256] = value

    def value_stage(index):
        h, n, at = blocks[index]
        rows, k_range, lanes, _ = parts_of(blocks[index])
        out = dot(keys_turned[lanes, k_range], probs[n][h % 2, :, at : at + 256], NN)
        out = jnp.where(low_lane, 0.0, dot(turn, out.astype(bf16), NT))
        heads[rows, lanes] = out.astype(bf16)
        if index + 1 == len(blocks) or blocks[index + 1][0] != h:
            for copy in prob_copies(h):
                copy.start()

    score_stage(0)
    for index in range(len(blocks)):
        if index + 1 < len(blocks):
            score_stage(index + 1)
        if index:
            value_stage(index - 1)
        softmax_stage(index)
    value_stage(len(blocks) - 1)
    send_out(heads, heads_ref)
    for g in range(GROUPS):
        for kind, ref in ((1, fc_one), (2, fc_two)):
            for j in range(D // TR):
                row = g * D + j * TR
                ref[row : row + TR, 0:D] = tile_of(g, kind * 20 + j)

    for copy in copies[held_count + 1 :]:
        copy.wait()
    for at in range(0, HALF, 256):
        rows = slice(at, at + 256)
        before = jnp.where(mask, second[rows, :] + vec[32:33, :], 0.0)
        second[rows, :] = before + dot(heads[rows, :], table[1], NN)

    kept = {}

    def norm_stage(n):
        rows = slice(n * 256, n * 256 + 256)
        normed, scale = norm_parts(second[rows, :], mask)
        mlp_in[rows, :] = (normed * vec[33:34, :] + vec[34:35, :]).astype(bf16)
        kept[n] = normed, scale

    def pre_stage(t):
        rows = slice(t // 5 * 256, t // 5 * 256 + 256)
        lanes = slice(t % 5 * 256, t % 5 * 256 + 256)
        pres[t % 3] = dot(mlp_in[rows, :], fc_one[lanes, :], NT)
        backs[t % 3] = dot(cot_low[rows, :], fc_two[lanes, :], NT)

    def gelu_stage(t):
        lanes = slice(t % 5 * 256, t % 5 * 256 + 256)
        total = jnp.zeros((8, 256), f32)
        for r in range(0, 256, 16):
            rows = slice(t // 5 * 256 + r, t // 5 * 256 + r + 16)
            pre = pres[t % 3, r : r + 16] + bias_one[:, lanes]
            below, density = phi_parts(pre)
            hidden[rows, lanes] = (pre * below).astype(bf16)
            back = backs[t % 3, r : r + 16] * (below + pre * density)
            back_low = back.astype(bf16)
            grad_pre[rows, lanes] = back_low
            back = back_low.astype(f32)
            total = total + (back[0:8] + back[8:16])
        fc_rows[:, lanes] += total

    def result_stage(n):
        rows = slice(n * 256, n * 256 + 256)
        normed, scale = kept.pop(n)
        cot_wide = cot_low[rows, :].astype(f32)
        result = second[rows, :] + dot(hidden[rows, :], fc_two[...], NN) + vec[39:40, :]
        block_out[rows, :] = jnp.where(mask, result, 0.0).astype(bf16)
        grad_in = dot(grad_pre[rows, :], fc_one[...], NN)
        rows_out[33:34, :] += jnp.sum(grad_in * normed, axis=0, keepdims=True)
        rows_out[34:35, :] += jnp.sum(grad_in, axis=0, keepdims=True)
        rows_out[39:40, :] += jnp.sum(cot_wide, axis=0, keepdims=True)
        whole = cot_wide + norm_back(grad_in, normed, scale, vec[33:34, :])
        low = jnp.where(mask, whole, 0.0).astype(bf16)
        branch[rows, :] = low
        rows_out[32:33, :] += jnp.sum(low.astype(f32), axis=0, keepdims=True)
        rows = pl.ds(n * 256, 256)
        send_out(branch.at[rows], branch_ref.at[rows])
        send_out(block_out.at[rows], block_ref.at[rows])

    norm_stage(0)
    pre_stage(0)
    for t in range(20):
        if t + 1 < 20:
            if (t + 1) % 5 == 0:
                norm_stage((t + 1) // 5)
            pre_stage(t + 1)
        gelu_stage(t)
        if t % 5 == 0 and t:
            result_stage(t // 5 - 1)
    result_stage(3)
    for kind, (left, right) in enumerate(((grad_pre, mlp_in), (hidden, cot_low))):
        value = dot(left[...], right[...], TN)
        rows = slice(kind * D, kind * D + D)
        for g in range(GROUPS):
            at = jnp.bitwise_xor(part, g)
            piece = value[g * D : g * D + D].astype(bf16)
            grads[lax.rem(at, 2), lax.div(at, 2), rows] = piece
        rows = pl.ds(kind * D, D)
        send_out(grads.at[1, :, rows], send_ref.at[:, rows])
        send_out(grads.at[0, :, rows], keep_ref.at[:, rows])
    for copy in outs + prob_copies(HEADS - 2) + prob_copies(HEADS - 1):
        copy.wait()


def forward_block(
    meta, attend, first, vec, bias_qv, bias_one, cot_own, cot_oth, held, places_of, ranks
):
    owned = SLOTS // ranks
    probs = [(HEADS,) + shape for shape in PROBS]
    shapes = probs + [
        (1792, HEAD_LANES),
        (HALF, HEAD_LANES),
        (HALF, HEAD_LANES),
        (2, HEAD_LANES, DP),
        (HALF, DP),
        (HALF, DP),
        (2, 2 * D, DP),
        (2, 2 * D, DP),
    ]
    return pl.pallas_call(
        functools.partial(forward_kernel, places_of),
        out_shape=[jax.ShapeDtypeStruct(shape, bf16) for shape in shapes]
        + [jax.ShapeDtypeStruct((NVEC, DP), f32), jax.ShapeDtypeStruct((8, FF), f32)],
        in_specs=[SMEM, ANY, ANY, VMEM, VMEM, VMEM, VMEM, VMEM] + [LOOSE] * len(held),
        out_specs=[ANY] * 11 + [VMEM] * 2,
        scratch_shapes=[pltpu.VMEM((2,) + shape, bf16) for shape in PROBS]
        + [pltpu.VMEM(shape, bf16) for shape in shapes[3:9]]
        + [
            pltpu.VMEM((2, 2, 2 * D, DP), bf16),
            pltpu.VMEM((3, 1024, 256), f32),
            pltpu.VMEM((3, 256, 256), f32),
            pltpu.VMEM((3, 256, 256), f32),
            pltpu.VMEM((HALF, DP), f32),
            pltpu.VMEM((GROUPS, ranks, owned, TR, D), bf16),
            pltpu.VMEM((FF, DP), bf16),
            pltpu.VMEM((FF, DP), bf16),
            pltpu.VMEM((HALF, FF), bf16),
            pltpu.VMEM((HALF, FF), bf16),
            pltpu.VMEM((HALF, DP), bf16),
            pltpu.VMEM((HALF, DP), bf16),
            pltpu.VMEM((SEQ, DP), bf16),
            pltpu.VMEM((HEAD_LANES, 1792), bf16),
            pltpu.SemaphoreType.DMA((2 * len(held) + 4,)),
            pltpu.SemaphoreType.DMA((2, 3)),
            pltpu.SemaphoreType.DMA((16,)),
        ],
        compiler_params=pltpu.CompilerParams(vmem_limit_bytes=54 * 2**20),
        cost_estimate=cost(30),
        name="forward_block",
    )(meta, attend, first, vec, bias_qv, bias_one, cot_own, cot_oth, *held)


def backward_kernel(
    meta,
    attend_ref,
    prob_ra,
    prob_rb,
    prob_rc,
    keys_in,
    query_in,
    heads_in,
    table_ref,
    branch_ref,
    attend_out,
    send_ref,
    keep_ref,
    bias_rows,
    prob_a,
    prob_b,
    prob_c,
    keys,
    query,
    heads,
    grad_heads,
    mixed_keys,
    mixed_query,
    turned_scores,
    attend_own,
    grads,
    attend,
    table,
    branch,
    keys_turned,
    wide,
    grad_attend,
    sem,
    in_sem,
    out_sem,
):
    probs = (prob_a, prob_b, prob_c)

    def head_copies(h):
        pairs = [(s.at[h], p.at[h % 3]) for s, p in zip((prob_ra, prob_rb, prob_rc), probs)]
        lanes = pl.ds(h * 128, 128)
        for source, buf in ((keys_in, keys), (query_in, query), (heads_in, heads)):
            pairs.append((source.at[:, lanes], buf.at[:, lanes]))
        return [
            pltpu.make_async_copy(source, buf, sem.at[h % 2, n])
            for n, (source, buf) in enumerate(pairs)
        ]

    copies = [
        pltpu.make_async_copy(source, buf, in_sem.at[n])
        for n, (source, buf) in enumerate(
            ((table_ref, table), (branch_ref, branch), (attend_ref, attend))
        )
    ]
    for copy in copies[:2] + head_copies(0):
        copy.start()
    core, clips = layout_of(meta)
    part = meta[0]
    pieces = own_pieces(core, clips)
    turn = identity(256, 256)
    small_turn = identity(128, 128)
    ones = jnp.ones((8, 128), bf16)
    low_lanes = (lax.broadcasted_iota(jnp.int32, (1, HEAD_LANES), 1) & 127) < HD
    low_lane = low_lanes[:, 0:128]
    for copy in copies[:2]:
        copy.wait()
    for at in range(0, HALF, 256):
        rows = slice(at, at + 256)
        value = dot(branch[rows, :], table[1], NT)
        grad_heads[rows, :] = jnp.where(low_lanes, 0.0, value).astype(bf16)
    other_small = pl.ds(mult(1536 + (1 - core) * 256, 256), 256)
    mixed_keys[other_small, :] = jnp.zeros((256, HEAD_LANES), bf16)

    blocks = [
        (h, n, at)
        for h in range(HEADS)
        for n in range(3)
        for at in range(0, SEGMENTS[n][1], 256)
    ]
    inners = {}

    def head_stage(h):
        lanes = slice(h * 128, h * 128 + 128)
        for copy in head_copies(h):
            copy.wait()
        for copy in head_copies(h + 1) if h + 1 < HEADS else copies[2:]:
            copy.start()
        keys_turned[h % 2] = dot(small_turn, keys[:, lanes], NT).astype(bf16)
        out_wide = grad_heads[:, lanes].astype(f32)
        high, low = two_parts(out_wide * heads[:, lanes].astype(f32))
        inners[h] = (dot(ones, high, NT) + dot(ones, low, NT))[0:1]
        bias_rows[h] = jnp.sum(out_wide, axis=0, keepdims=True)

    def parts_of(block):
        h, n, at = block
        q_at, _, k_at, k_rows = SEGMENTS[n]
        lanes = slice(h * 128, h * 128 + 128)
        return slice(q_at + at, q_at + at + 256), slice(k_at, k_at + k_rows), lanes, k_rows

    def probs_stage(index):
        rows, k_range, lanes, k_rows = parts_of(blocks[index])
        if index == 0 or blocks[index - 1][0] != blocks[index][0]:
            head_stage(blocks[index][0])
        wide[index % 3, 0:k_rows] = dot(keys[k_range, lanes], grad_heads[rows, lanes], NT)

    def scores_stage(index):
        h, n, at = blocks[index]
        rows, _, _, k_rows = parts_of(blocks[index])
        for r in range(0, k_rows, 32):
            weights = probs[n][h % 3, r : r + 32, at : at + 256].astype(f32)
            value = (weights * (wide[index % 3, r : r + 32] - inners[h][:, rows])).astype(bf16)
            turned_scores[n, r : r + 32, at : at + 256] = value

    def query_stage(index):
        h, n, at = blocks[index]
        rows, k_range, lanes, k_rows = parts_of(blocks[index])
        value = dot(keys_turned[h % 2, :, k_range], turned_scores[n, 0:k_rows, at : at + 256], NN)
        value = dot(turn, (value * 0.125).astype(bf16), NT)
        value = jnp.where(low_lane, value, 0.0)
        mixed_query[rows, lanes] = value.astype(bf16)
        bias_rows[h] += jnp.sum(value, axis=0, keepdims=True)
        q_at, q_rows, k_at, _ = SEGMENTS[n]
        if at + 256 < q_rows:
            return
        rows = slice(q_at, q_at + q_rows)
        both = dot(query[rows, lanes], turned_scores[n, 0:k_rows, 0:q_rows], TT)
        both = both + dot(grad_heads[rows, lanes], probs[n][h % 3], TT)
        both = jnp.transpose(both)
        if n == 2:
            k_range = pl.ds(mult(1536 + core * 256, 256), 256)
        mixed_keys[k_range, lanes] = both.astype(bf16)

    probs_stage(0)
    for index in range(len(blocks)):
        if index + 1 < len(blocks):
            probs_stage(index + 1)
        if index:
            query_stage(index - 1)
        scores_stage(index)
    query_stage(len(blocks) - 1)

    copies[2].wait()
    for count, at, canon, _ in pieces:
        attend_own[at : at + count, :] = attend[pl.ds(mult(canon, 256), count), :]
    outs = []

    def send_out(source, target):
        outs.append(pltpu.make_async_copy(source, target, out_sem.at[len(outs)]))
        outs[-1].start()

    grad_attend[other_small, :] = jnp.zeros((256, DP), bf16)
    for n, (count, at, canon, _) in enumerate(pieces):
        own_rows = pl.ds(mult(canon, 256), count)
        value = dot(mixed_keys[own_rows, :], table[0], NN)
        value = value + dot(mixed_query[at : at + count, :], table[1], NN)
        grad_attend[own_rows, :] = value.astype(bf16)
        if n < 2:
            other_rows = pl.ds(mult(CANON[n] + (1 - core) * count, 256), count)
            value = dot(mixed_keys[other_rows, :], table[0], NN)
            grad_attend[other_rows, :] = value.astype(bf16)
            rows = pl.ds(CANON[n], SIZES[n])
        else:
            rows = pl.ds(1536, 512)
        send_out(grad_attend.at[rows], attend_out.at[rows])
    sides = (
        dot(mixed_query[...], attend_own[...], TN) + dot(heads[...], branch[...], TN),
        dot(mixed_keys[...], attend[...], TN),
    )
    for g in range(GROUPS):
        at = jnp.bitwise_xor(part, g)
        for r in range(5):
            side, row = table_place(g * 5 + r)
            value = sides[1 - side][row : row + 64].astype(bf16)
            grads[lax.rem(at, 2), lax.div(at, 2), r * 64 : r * 64 + 64] = value
    send_out(grads.at[1], send_ref)
    send_out(grads.at[0], keep_ref)
    for copy in outs:
        copy.wait()


def backward_block(meta, attend, probs, keys, query, heads, table, branch):
    return pl.pallas_call(
        backward_kernel,
        out_shape=(
            jax.ShapeDtypeStruct((SEQ, DP), bf16),
            jax.ShapeDtypeStruct((2, D, DP), bf16),
            jax.ShapeDtypeStruct((2, D, DP), bf16),
            jax.ShapeDtypeStruct((HEADS, 1, 128), f32),
        ),
        in_specs=[SMEM] + [ANY] * 9,
        out_specs=(LOOSE, LOOSE, LOOSE, VMEM),
        scratch_shapes=[pltpu.VMEM((3,) + shape, bf16) for shape in PROBS]
        + [
            pltpu.VMEM((1792, HEAD_LANES), bf16),
            pltpu.VMEM((HALF, HEAD_LANES), bf16),
            pltpu.VMEM((HALF, HEAD_LANES), bf16),
            pltpu.VMEM((HALF, HEAD_LANES), bf16),
            pltpu.VMEM((SEQ, HEAD_LANES), bf16),
            pltpu.VMEM((HALF, HEAD_LANES), bf16),
            pltpu.VMEM((3, 1024, 512), bf16),
            pltpu.VMEM((HALF, DP), bf16),
            pltpu.VMEM((2, 2, D, DP), bf16),
            pltpu.VMEM((SEQ, DP), bf16),
            pltpu.VMEM((2, HEAD_LANES, DP), bf16),
            pltpu.VMEM((HALF, DP), bf16),
            pltpu.VMEM((2, 128, 1792), bf16),
            pltpu.VMEM((3, 1024, 256), f32),
            pltpu.VMEM((SEQ, DP), bf16),
            pltpu.SemaphoreType.DMA((2, 6)),
            pltpu.SemaphoreType.DMA((3,)),
            pltpu.SemaphoreType.DMA((5,)),
        ],
        compiler_params=pltpu.CompilerParams(vmem_limit_bytes=56 * 2**20),
        cost_estimate=cost(16),
        name="backward_block",
    )(meta, attend, *probs, keys, query, heads, table, branch)


def owner_of(i, b):
    if i == 0:
        return b // 2, b % 2 * 256
    return (b, 512) if i == 1 else (i - 2, 768)


def norm_back_kernel(
    meta, own, other, second_own, second_oth, first, vec, rows_mlp, fc_rows, bias_rows, grad, rows_out
):
    core, clips = layout_of(meta)
    rows_out[...] = rows_mlp[...]
    for h in range(HEADS):
        rows_out[30:31, h * HD : h * HD + HD] = bias_rows[h][:, 0:HD]
        rows_out[31:32, h * HD : h * HD + HD] = bias_rows[h][:, HD:]
    for g in range(GROUPS):
        total = jnp.sum(fc_rows[:, g * D : g * D + D], axis=0, keepdims=True)
        rows_out[35 + g : 36 + g, 0:D] = total
    mask = lax.broadcasted_iota(jnp.int32, (1, DP), 1) < D
    for i in range(4):
        for b in range(SIZES[i] // 256):
            place = clips[i][0] + b * 256
            owner, at = owner_of(i, b)
            rows = slice(CANON[i] + b * 256, CANON[i] + b * 256 + 256)
            reach = (place >= core * HALF - 512) & (place < core * HALF + HALF + 512)

            @pl.when(reach)
            def _(place=place, owner=owner, at=at, rows=rows):
                grad_out = own[rows, :].astype(f32) + other[rows, :].astype(f32)
                normed, scale = norm_parts(first[rows, :], mask)
                second = jnp.where(
                    core == owner, second_own[at : at + 256, :], second_oth[at : at + 256, :]
                )
                whole = second.astype(f32) + norm_back(grad_out, normed, scale, vec[28:29, :])
                grad[rows, :] = whole

                @pl.when(lax.div(place, HALF) == core)
                def _():
                    rows_out[27:28, :] += jnp.sum(whole, axis=0, keepdims=True)
                    rows_out[28:29, :] += jnp.sum(grad_out * normed, axis=0, keepdims=True)
                    rows_out[29:30, :] += jnp.sum(grad_out, axis=0, keepdims=True)


def norm_backward(meta, own, other, second_own, second_oth, first, vec, rows):
    return pl.pallas_call(
        norm_back_kernel,
        out_shape=(
            jax.ShapeDtypeStruct((SEQ, DP), f32),
            jax.ShapeDtypeStruct((NVEC, DP), f32),
        ),
        in_specs=[SMEM] + [VMEM] * 9,
        out_specs=(VMEM,) * 2,
        compiler_params=pltpu.CompilerParams(vmem_limit_bytes=20 * 2**20),
        cost_estimate=cost(8),
        name="norm_backward",
    )(meta, own, other, second_own, second_oth, first, vec, *rows)


def conv_back_kernel(meta, grad, x_own, vec, rows_in, grad_rows, rows_out, padded, xw, vb):
    core, clips = layout_of(meta)
    clear_gaps(padded)
    tap_rows(vec, vb)
    turn = identity(256, 256)
    rows_out[...] = rows_in[...]
    for b in range(4):
        put_rows(xw, b * 32, dot(turn, x_own[:, b * 256 : b * 256 + 256], NT))
    for i in range(4):
        for b in range(SIZES[i] // 256):
            at = CANON[i] + b * 256
            put_rows(padded, PTILES[i] + b * 32, grad[at : at + 256, :])
    blocks = [block_of(clips, core * HALF + b * 256) for b in range(4)]
    for c in range(3):
        sums = tuple(jnp.zeros((8, 128), f32) for _ in range(27))
        for b, (width, plane, local, tile) in enumerate(blocks):
            not_last, not_first = columns(2, width)

            def step(n, sums, b=b, c=c, block=blocks[b], not_last=not_last, not_first=not_first):
                width, plane, local, tile = block
                sums = list(sums)
                x = xw[c, pl.ds(b * 32 + n * 2, 2)]
                shifted = (to_right(x, not_last), x, to_left(x, not_first))
                parts = [None] * 3
                at = tile + n * 2
                for k, value in neighbours(padded, c, at, 2, width, plane, local + n * 2):
                    for dc in range(3):
                        mirror = 26 - (k + dc)
                        term = value * vb[mirror, c]
                        parts[dc] = term if parts[dc] is None else parts[dc] + term
                        product = value * shifted[dc]
                        sums[mirror] = sums[mirror] + (product[0] + product[1])
                total = padded[c, pl.ds(at, 2)] + parts[1]
                total = total + to_left(parts[0], not_first)
                total = total + to_right(parts[2], not_last)
                rows = pl.ds(mult(b * 256 + n * 16, 16), 16)
                grad_rows[rows, c * 128 : c * 128 + 128] = total.reshape(16, 128).astype(bf16)
                return tuple(sums)

            sums = lax.fori_loop(0, 16, step, sums)
        for k in range(27):
            lanes = slice(c * 128, c * 128 + 128)
            rows_out[k : k + 1, lanes] = jnp.sum(sums[k], axis=0, keepdims=True)


def conv_backward(meta, grad, x_own, vec, rows):
    return pl.pallas_call(
        conv_back_kernel,
        out_shape=(
            jax.ShapeDtypeStruct((HALF, DP), bf16),
            jax.ShapeDtypeStruct((NVEC, DP), f32),
        ),
        in_specs=[SMEM] + [VMEM] * 4,
        out_specs=(VMEM,) * 2,
        scratch_shapes=[
            pltpu.VMEM((3, ALL_TILES, 8, 128), f32),
            pltpu.VMEM((3, HALF // 8, 8, 128), f32),
            pltpu.VMEM((27, 3, 8, 128), f32),
        ],
        compiler_params=pltpu.CompilerParams(vmem_limit_bytes=20 * 2**20),
        cost_estimate=cost(11),
        name="conv_backward",
    )(meta, grad, x_own, vec, rows)


def turn_block_kernel(meta, out_own, out_oth, block_out):
    core, clips = layout_of(meta)
    turn = identity(D, DP)
    for i in range(4):
        for b in range(SIZES[i] // 256):
            place = clips[i][0] + b * 256
            owner, at = owner_of(i, b)
            mine = lax.div(place, HALF) == core
            lanes = pl.ds(mult(lax.rem(place, HALF), 256), 256)
            for source, here in ((out_own, core == owner), (out_oth, core != owner)):

                @pl.when(mine & here)
                def _(source=source, at=at, lanes=lanes):
                    block_out[:, lanes] = dot(turn, source[at : at + 256, :], NT).astype(bf16)


def turn_grad_kernel(grad_rows, input_grad):
    turn = identity(D, DP)
    mask = lax.broadcasted_iota(jnp.int32, (1, DP), 1) < D
    for b in range(4):
        rows = slice(b * 256, b * 256 + 256)
        value = jnp.where(mask, grad_rows[rows, :].astype(f32), 0.0).astype(bf16)
        input_grad[:, rows] = dot(turn, value, NT).astype(bf16)


def turned_block(meta, out_own, out_oth):
    return pl.pallas_call(
        turn_block_kernel,
        out_shape=jax.ShapeDtypeStruct((D, HALF), bf16),
        in_specs=[SMEM] + [VMEM] * 2,
        out_specs=VMEM,
        compiler_params=pltpu.CompilerParams(vmem_limit_bytes=8 * 2**20),
        cost_estimate=cost(2),
        name="turned_block",
    )(meta, out_own, out_oth)


def turned_grad(grad_rows):
    return pl.pallas_call(
        turn_grad_kernel,
        out_shape=jax.ShapeDtypeStruct((D, HALF), bf16),
        in_specs=[VMEM],
        out_specs=VMEM,
        compiler_params=pltpu.CompilerParams(vmem_limit_bytes=8 * 2**20),
        cost_estimate=cost(2),
        name="turned_grad",
    )(grad_rows)


def spread_kernel(meta, fc_keep, fc_recv, table_keep, table_recv, *refs):
    slots = refs[-1]
    outs = refs[:-1]
    _, ranks, owned = slots.shape[:3]
    slots[...] = jnp.zeros_like(slots)
    for far in range(2):
        for first_tile, count, keep, recv in (
            (0, D // TR, table_keep, table_recv),
            (D // TR, 2 * D // TR, fc_keep, fc_recv),
        ):

            for j in range(count):
                rows = slice(j * TR, j * TR + TR)
                value = keep[far, rows, :].astype(f32) + recv[far, rows, :].astype(f32)
                slot = meta[META_TILES + first_tile + j]
                slots[far, lax.div(slot, owned), lax.rem(slot, owned)] = value[:, 0:D]
    cut = owned - owned // 2
    outs[0][...] = slots[0, :, 0:cut]
    outs[1][...] = slots[1, :, 0:cut].astype(bf16)
    if cut < owned:
        outs[2][...] = slots[:, 0 : ranks // 2, cut:]
        outs[3][...] = slots[:, ranks // 2 :, cut:].astype(bf16)


def spread(meta, ranks, *grads):
    owned = SLOTS // ranks
    cut = owned - owned // 2
    shapes = [(ranks, cut, TR, D)]
    if cut < owned:
        shapes.append((2, ranks // 2, owned - cut, TR, D))
    out_shape = [jax.ShapeDtypeStruct(shape, kind) for shape in shapes for kind in (f32, bf16)]
    return pl.pallas_call(
        spread_kernel,
        out_shape=out_shape,
        in_specs=[SMEM] + [VMEM] * 4,
        out_specs=[VMEM] * len(out_shape),
        scratch_shapes=[pltpu.VMEM((2, ranks, owned, TR, D), f32)],
        compiler_params=pltpu.CompilerParams(vmem_limit_bytes=24 * 2**20),
        cost_estimate=cost(3),
        name="spread_tiles",
    )(meta, *grads)


def halves_kernel(count, *refs):
    for n in range(count):
        keep, recv = refs[2 * n], refs[2 * n + 1]
        out_keep, out_send = refs[2 * count + 2 * n], refs[2 * count + 2 * n + 1]
        half = keep.shape[0] // 2
        out_keep[...] = keep[0:half] + recv[0:half].astype(f32)
        out_send[...] = (keep[half:] + recv[half:].astype(f32)).astype(bf16)


def halves(pairs):
    flat = [value for pair in pairs for value in pair]
    out_shape = []
    for keep, _ in pairs:
        shape = (keep.shape[0] // 2,) + keep.shape[1:]
        out_shape += [jax.ShapeDtypeStruct(shape, f32), jax.ShapeDtypeStruct(shape, bf16)]
    return pl.pallas_call(
        functools.partial(halves_kernel, len(pairs)),
        out_shape=out_shape,
        in_specs=[VMEM] * len(flat),
        out_specs=[VMEM] * len(out_shape),
        compiler_params=pltpu.CompilerParams(vmem_limit_bytes=16 * 2**20),
        cost_estimate=cost(1.5),
        name="halves",
    )(*flat)


def paired_sum(values):
    while len(values) > 1:
        values = [values[n] + values[n + 1] for n in range(0, len(values), 2)]
    return values[0]


def sent_vector(value, owned):
    rows = value[0, owned : owned + VECTOR_TILES].astype(f32).reshape(VECTOR_TILES * TR, D)
    return rows[:NVEC]


def split_kernel(counts, vectors, *refs):
    terms, rest = refs[: sum(counts)], refs[sum(counts) :]
    own_vectors, outs, vector_out = rest[:vectors], rest[vectors:-1], rest[-1]
    size, owned = outs[0].shape[:2]
    values = [ref[:, 0:D] for ref in own_vectors]
    if vectors == 1:
        values += [sent_vector(ref, owned) for ref in terms[1:]]
    spare = jnp.zeros((VECTOR_TILES * TR - NVEC, D), f32)
    total = jnp.concatenate([paired_sum(values), spare], axis=0).astype(bf16)
    vector_out[...] = jnp.zeros_like(vector_out)
    vector_out[:, 0:D] = total.astype(f32)[:NVEC]
    for q, out in enumerate(outs):
        at, first = 0, 0
        for count in counts:
            rows = slice(q * size, q * size + size)
            value = terms[at][rows]
            width = value.shape[1]
            for other in terms[at + 1 : at + count]:
                value = value + other[rows, 0:width].astype(f32)
            out[:, first : first + width] = value.astype(out.dtype)
            at, first = at + count, first + width
        if q:
            for n in range(size):
                out[n, owned:] = total.reshape(VECTOR_TILES, TR, D)


def split(groups, vectors, pieces):
    flat = [value for group in groups for value in group]
    owned = sum(group[0].shape[1] for group in groups)
    size = flat[0].shape[0] // pieces
    out_shape = [jax.ShapeDtypeStruct((size, owned, TR, D), f32)]
    sent = jax.ShapeDtypeStruct((size, owned + VECTOR_TILES, TR, D), bf16)
    out_shape += [sent] * (pieces - 1) + [jax.ShapeDtypeStruct((NVEC, DP), f32)]
    return pl.pallas_call(
        functools.partial(split_kernel, tuple(len(group) for group in groups), len(vectors)),
        out_shape=out_shape,
        in_specs=[VMEM] * (len(flat) + len(vectors)),
        out_specs=[VMEM] * len(out_shape),
        compiler_params=pltpu.CompilerParams(vmem_limit_bytes=16 * 2**20),
        cost_estimate=cost(1.5),
        name="split_slots",
    )(*flat, *vectors)


def dot_parts(a, b, dims):
    return dot(a[0], b[0], dims) + (dot(a[1], b[0], dims) + dot(a[0], b[1], dims))


def dot_low(a, b, dims):
    rows = a.shape[0]
    both = dot(jnp.concatenate(two_parts(a), axis=0), b, dims)
    return both[:rows] + both[rows:]


def bases_kernel(left, right, left_out, right_out):
    owned = left.shape[0]
    rows = owned * TR
    at = [lax.broadcasted_iota(jnp.int32, (TR, rows), n) for n in range(2)]
    repeat = jnp.where(at[0] == (at[1] & (TR - 1)), 1.0, 0.0).astype(bf16)
    at = [lax.broadcasted_iota(jnp.int32, (rows, rows), n) // TR for n in range(2)]
    for n, piece in enumerate(two_parts(left[...].reshape(rows, TR))):
        left_out[n] = jnp.where(at[0] == at[1], dot(piece, repeat, NN), 0.0).astype(bf16)
    right_out[...] = right[...].astype(bf16)


def split_bases(left, right):
    owned = left.shape[0]
    return pl.pallas_call(
        bases_kernel,
        out_shape=(
            jax.ShapeDtypeStruct((2, owned * TR, owned * TR), bf16),
            jax.ShapeDtypeStruct(right.shape, bf16),
        ),
        in_specs=[VMEM] * 2,
        out_specs=(VMEM,) * 2,
        compiler_params=pltpu.CompilerParams(vmem_limit_bytes=24 * 2**20),
        cost_estimate=cost(3),
        name="split_bases",
    )(left, right)


def soap_kernel(count, corr, *refs):
    grads, refs = refs[:count], refs[count:]
    vector_grad, vectors, vector_first, vector_second = refs[:4]
    masters, left, right, first, second, out_w, out_m, out_v = refs[4:12]
    new_vectors, new_vector_first, new_vector_second, wide = refs[12:]
    grad = grads[0][0]
    owned = grad.shape[0]
    rows = owned * TR
    for other in grads[1:]:
        grad = grad + other[0, 0:owned].astype(f32)
    sides = (left[0], left[1])
    turned = dot_parts(sides, two_parts(grad.reshape(rows, D)), TN)

    def moments(old_first, old_second, value):
        new_first = beta_one * old_first + (1.0 - beta_one) * value
        new_second = beta_two * old_second + (1.0 - beta_two) * value * value
        direction = new_first / corr[0] / (jnp.sqrt(new_second / corr[1]) + adam_eps)
        return new_first, new_second, direction

    for s in range(owned):
        rotated = dot_low(turned[s * TR : s * TR + TR], right[s], NN)
        out_m[s], out_v[s], direction = moments(first[s], second[s], rotated)
        wide[s * TR : s * TR + TR] = dot_low(direction, right[s], NT)
    back = dot_parts(sides, two_parts(wide[...]), NN).reshape(owned, TR, D)
    out_w[...] = masters[...] - matrix_rate * (back + matrix_decay * masters[...])
    value = paired_sum([vector_grad[:, 0:D]] + [sent_vector(ref, owned) for ref in grads[1:]])
    new_first, new_second, direction = moments(vector_first[...], vector_second[...], value)
    new_vector_first[...] = new_first
    new_vector_second[...] = new_second
    new_vectors[...] = vectors[...] - vector_rate * direction


def soap(corr, grads, vectors, masters, bases, first, second):
    shape = jax.ShapeDtypeStruct(masters.shape, f32)
    vector = jax.ShapeDtypeStruct((NVEC, D), f32)
    return pl.pallas_call(
        functools.partial(soap_kernel, len(grads)),
        out_shape=(shape, shape, shape, vector, vector, vector),
        in_specs=[SMEM] + [VMEM] * (len(grads) + 9),
        out_specs=(VMEM,) * 6,
        scratch_shapes=[pltpu.VMEM((masters.shape[0] * TR, D), f32)],
        compiler_params=pltpu.CompilerParams(vmem_limit_bytes=24 * 2**20),
        cost_estimate=cost(5),
        name="tile_update",
    )(corr, *grads, *vectors, masters, *bases, first, second)


def flipped(value, axes, bit):
    size = lax.axis_size(axes)
    return lax.ppermute(value, axes, [(i, i ^ bit) for i in range(size)])


def tied(*values):
    return lax.optimization_barrier(values)


def masks_of(bits):
    return [0, bits[0]] if len(bits) == 1 else [0, bits[1], bits[0], bits[0] | bits[1]]


def on_device(
    block_input,
    cotangent,
    clip_starts,
    clip_shapes,
    tile_slot,
    masters,
    left_bases,
    right_bases,
    first_moment,
    second_moment,
    vectors,
    vector_first,
    vector_second,
    step_count,
):
    part = lax.axis_index("tp")
    rank = lax.axis_index("dp")
    ranks, groups = lax.axis_size("dp"), lax.axis_size("tp")
    bits = [1 << n for n in range(ranks.bit_length() - 1)]
    near, far = bits[0], [tuple(bits[n : n + 2]) for n in range(1, len(bits), 2)]
    owned = masters.shape[1]
    cut = owned - owned // 2

    relative = jnp.bitwise_xor(tile_slot // owned, rank)
    position = sum(
        ((relative >> n) & 1) << (len(bits) - 1 - n) for n in range(len(bits))
    ) * owned + tile_slot % owned
    meta = jnp.concatenate(
        [part[None].astype(jnp.int32), clip_starts.reshape(-1), clip_shapes.reshape(-1), position]
    )
    vec = jnp.pad(vectors, ((0, 0), (0, DP - D)))
    vec = vec.at[29, D].set(1.0).at[34, D].set(1.0)
    bias_qv = jnp.concatenate(
        [vectors[30].reshape(HEADS, HD), vectors[31].reshape(HEADS, HD)], axis=1
    ).reshape(1, HEAD_LANES)
    bias_one = vectors[35:39].reshape(1, FF)

    x_own = block_input.T
    cot_own = cotangent.T
    x_oth = flipped(x_own, "tp", 1)
    cot_oth = flipped(cot_own, "tp", 1)
    held = masters[0].astype(bf16)[None]
    for group in reversed(far):
        held = jnp.concatenate([flipped(held, "dp", m) if m else held for m in masks_of(group)])
    held, meta, vec, bias_qv, bias_one, x_oth = tied(held, meta, vec, bias_qv, bias_one, x_oth)
    near_first = held[:, :cut]
    near_first = jnp.stack([near_first, flipped(near_first, "dp", near)])
    early = [(0, ((0, 0), (0, 1)), near_first)]
    late = [(0, ((2, 0), (2, 1)), flipped(near_first, "tp", 2))]
    if cut < owned:
        far_first = held[:, cut:]
        far_first = jnp.stack([far_first, flipped(far_first, "tp", 2)])
        early.append((cut, ((0, 0), (2, 0)), far_first))
        late.append((cut, ((0, 1), (2, 1)), flipped(far_first, "dp", near)))
    attend, first = conv_forward(meta, x_own, x_oth, vec, early[-1][2])
    attend, *values = tied(attend, *[value for _, _, value in late])
    pieces = early + [(low, entries, value) for (low, entries, _), value in zip(late, values)]
    for low, entries, value in list(pieces):
        entries = tuple((q + 1, side) for q, side in entries)
        pieces.append((low, entries, flipped(value, "tp", 1)))

    (
        prob_a,
        prob_b,
        prob_c,
        keys,
        query,
        heads,
        table,
        block_out,
        branch,
        fc_send,
        fc_keep,
        rows_mlp,
        fc_rows,
    ) = forward_block(
        meta,
        attend,
        first,
        vec,
        bias_qv,
        bias_one,
        cot_own,
        cot_oth,
        [value for _, _, value in pieces],
        tuple((low, entries) for low, entries, _ in pieces),
        ranks,
    )
    block_oth = flipped(block_out, "tp", 1)
    branch_oth = flipped(branch, "tp", 1)
    fc_recv = flipped(fc_send, "tp", 1)
    grad_attend, table_send, table_keep, bias_rows = backward_block(
        meta, attend, (prob_a, prob_b, prob_c), keys, query, heads, table, branch
    )
    grad_attend, table_send, block_oth, branch_oth, fc_recv, left, right = tied(
        grad_attend, table_send, block_oth, branch_oth, fc_recv, left_bases[0], right_bases[0]
    )
    grad_attend_oth = flipped(grad_attend, "tp", 1)
    table_recv = flipped(table_send, "tp", 1)
    bases = split_bases(left, right)
    table_recv, *bases = tied(table_recv, *bases)

    spreads = spread(meta, ranks, fc_keep, fc_recv, table_keep, table_recv)
    pairs = [(spreads[0], flipped(spreads[1], "tp", 2))]
    if cut < owned:
        pairs.append((spreads[2], flipped(spreads[3], "dp", near)))
    grad_first, vector_rows = norm_backward(
        meta,
        grad_attend,
        grad_attend_oth,
        branch,
        branch_oth,
        first,
        vec,
        (rows_mlp, fc_rows, bias_rows),
    )
    grad_rows, vector_grad = conv_backward(meta, grad_first, x_own, vec, vector_rows)
    vector_grad, *recvs = tied(vector_grad, *[recv for _, recv in pairs])
    result = halves([(keep, recv) for (keep, _), recv in zip(pairs, recvs)])
    vector_oth = flipped(vector_grad, "tp", 1)
    terms = [(result[0], flipped(result[1], "dp", near))]
    if cut < owned:
        terms.append((result[2][0], flipped(result[3], "tp", 2)[0]))
    vector_grad, grad_rows, block_oth = tied(vector_grad + vector_oth, grad_rows, block_oth)
    vectors_near = [
        flipped(vector_grad, ("dp", "tp"), m) if m else vector_grad
        for m in masks_of((2, near * groups))
    ]
    input_grad = turned_grad(grad_rows)
    block_output = turned_block(meta, block_out, block_oth)
    for group in far:
        masks = masks_of(group)
        *sent, vector_own = split(terms, vectors_near, len(masks))
        terms = [tuple(flipped(v, "dp", m) if m else v for v, m in zip(sent, masks))]
        vectors_near = [vector_own]

    steps = step_count[0].astype(f32)
    corr_one = 1.0 - jnp.power(beta_one, steps)
    corr_two = 1.0 - jnp.power(beta_two, steps)
    new_masters, new_first, new_second, *new_vectors = soap(
        jnp.stack([corr_one, corr_two]),
        terms[0],
        (vector_own, vectors, vector_first, vector_second),
        masters[0],
        bases,
        first_moment[0],
        second_moment[0],
    )
    return (
        block_output.T,
        input_grad.T,
        new_masters[None],
        new_first[None],
        new_second[None],
        *new_vectors,
    )


def solution(mesh):
    tokens = P(("dp", "tp"), None)
    tiles = P("tp", "dp", None, None)
    in_specs = (
        tokens,
        tokens,
        P("dp", None),
        P("dp", None, None),
        P(),
        tiles,
        tiles,
        tiles,
        tiles,
        tiles,
        P(),
        P(),
        P(),
        P(),
    )
    out_specs = (tokens, tokens, tiles, tiles, tiles, P(), P(), P())
    return jax.shard_map(
        on_device, mesh=mesh, in_specs=in_specs, out_specs=out_specs, check_vma=False
    )
```
